128 devices in a mesh: rows: 64 (over y_lo, x, z, core), sub: 2 (over y_hi).
Axes of the slice: x: 4, y: 4 (y_hi: 2, y_lo: 2; y = y_hi * 2 + y_lo), z: 4, core: 2. Of those that a mesh axis runs over, the one named last changes fastest.
Arguments:
- matrix_rows: float32 [524288, 256], P(('rows', 'sub')), may hold values from -6 to 6
- signs: int32 [524288], P(('rows', 'sub')), may hold values from 0 to 1
- picks: int32 [128, 128, 4], P(('rows', 'sub')), may hold values from -1 to 4095, as said below
Outputs:
- mixed: float32 [524288, 256], P(('rows', 'sub'))
- panel: float32 [65536, 256], P(('rows', 'sub'))
- factor: float32 [256, 256], replicated
The draws below stay inside these ranges and needn't reach their ends.
Inputs may be any that keep to these rules, and one draw needn't show every extreme that they name: `picks`: -1 marks an empty slot; about half of the slots are filled.
All inputs are finite; a program needn't handle non-finite values.
Results may differ from the reference program's by a relative error of at most 0.000098.
Values sent between devices are 32-bit elements; how exact they have to be, the bound alone decides.
No kernel may reach another device: no remote copies, remote signals or barrier semaphores. Data moves between devices by JAX's collectives and lax.ppermute only.
A program may use at most 64 MiB of HBM per device.

```python
import math
import jax
import jax.numpy as jnp
from jax import lax

COLS = 256
LOCAL = 4096
CAP = 4
OWNERS = 128
TOTAL = 524288


def draw_picks(key, part):
    key = jax.random.fold_in(key, 7)
    first_key, second_key = jax.random.split(key)
    chosen = jax.random.randint(first_key, (OWNERS, OWNERS, CAP), 0, LOCAL)
    filled = jax.random.randint(second_key, (OWNERS, OWNERS, CAP), 0, 2)
    result = jnp.where(filled == 1, chosen, -1)
    result = result.at[0, 0, 0].set(LOCAL - 1)
    result = result.at[0, 0, 1].set(-1)
    return result.astype(jnp.int32)


def place_ends(drawn, own_key, smallest, largest):
    extent = drawn.shape
    place = [jax.random.randint(jax.random.fold_in(own_key, axis), (), 0, extent[axis]) for axis in range(len(extent))]
    drawn = drawn.at[tuple(place)].set(smallest)
    longest = extent.index(max(extent))
    place[longest] = (place[longest] + 1) % extent[longest]
    return drawn.at[tuple(place)].set(largest)


def level_of(own_key, dims, cuts, smallest, high):
    def one(position, blocks):
        draws = jax.random.uniform(jax.random.fold_in(jax.random.fold_in(own_key, 6), position), (blocks,), jnp.float32, smallest / len(cuts), high / len(cuts))
        return jnp.repeat(jnp.exp(draws), dims[position] // blocks).reshape((-1,) + (1,) * (len(dims) - position - 1))

    loudness = one(*cuts[0])
    for cut in cuts[1:]:
        loudness = loudness * one(*cut)
    return loudness


def gaussian(key, extent, deviation, bound, cuts=(), held_as=jnp.bfloat16):
    values = jax.random.normal(key, extent, jnp.float32) * deviation
    if len(cuts) > 0:
        values = level_of(key, extent, cuts, -0.22, 0.18) * values
    return jnp.clip(values, min=-bound, max=bound).astype(held_as)


def setup_inputs(seed: int = 0) -> dict:
    key_list = jax.random.split(jax.random.key(seed), 4)
    matrix_rows = gaussian(key_list[0], (TOTAL, COLS), 1.0, 6.0, ((0, 128),), jnp.float32)
    signs = place_ends(jax.random.randint(key_list[1], (TOTAL,), 0, 2), jax.random.fold_in(key_list[1], 1), 0, 1).astype(jnp.int32)
    picks = draw_picks(jax.random.fold_in(key_list[3], 71), 0)
    return dict(matrix_rows=matrix_rows, signs=signs, picks=picks)


def sylvester(order):
    row_index = lax.broadcasted_iota(jnp.int32, (order, order), 0)
    column_index = lax.broadcasted_iota(jnp.int32, (order, order), 1)
    correlation = jnp.bitwise_and(row_index, column_index)
    parity = jnp.zeros((order, order), jnp.int32)
    for level_bit in range(max(order.bit_length() - 1, 0)):
        parity = jnp.bitwise_xor(parity, jnp.bitwise_and(jnp.right_shift(correlation, level_bit), 1))
    return (1 - 2 * parity).astype(jnp.float32)

def reference(matrix_rows, signs, picks):
    flips = (2 * signs - 1).astype(jnp.float32) * (1.0 / math.sqrt(TOTAL))
    values = matrix_rows * flips[:, None]
    powers = LOCAL.bit_length() - 1
    first = 2 ** (powers // 2)
    second = LOCAL // first
    blocks = values.reshape(OWNERS, first, second, COLS)
    blocks = jnp.einsum('ij,djbc->dibc', sylvester(first), blocks, precision=lax.Precision.HIGHEST)
    blocks = jnp.einsum('ij,dajc->daic', sylvester(second), blocks, precision=lax.Precision.HIGHEST)
    blocks = jnp.einsum('ij,jabc->iabc', sylvester(OWNERS), blocks, precision=lax.Precision.HIGHEST)
    mixed = blocks.reshape(TOTAL, COLS)
    order_picks = jnp.transpose(picks, (1, 0, 2))
    sources = lax.broadcasted_iota(jnp.int32, order_picks.shape, 1)
    global_rows = sources * LOCAL + jnp.maximum(order_picks, 0)
    taken = jnp.take(mixed, global_rows.reshape(-1), axis=0)
    valid = order_picks.reshape(-1) >= 0
    panel = jnp.where(valid[:, None], taken, jnp.float32(0.0))
    expected = OWNERS * OWNERS * CAP / 2.0
    gram = jnp.dot(panel.T.astype(jnp.float32), panel.astype(jnp.float32), precision=lax.Precision.HIGHEST, preferred_element_type=jnp.float32) / expected
    factor = jnp.linalg.cholesky(gram).T
    return (mixed, panel, factor)
```

```python
import math

import jax
import jax.numpy as jnp
import numpy as np
from jax import lax
from jax.experimental import pallas as pl
from jax.experimental.pallas import tpu as pltpu
from jax.sharding import PartitionSpec as P

AXES = ("rows", "sub")
BLOCK = 256


def sylvester(order):
    matrix = np.ones((1, 1), np.float32)
    while matrix.shape[0] < order:
        matrix = np.block([[matrix, matrix], [matrix, -matrix]])
    return matrix


def butterflies(parts):
    count = len(parts)
    stride = 1
    while stride < count:
        for low in range(count):
            if low & stride == 0:
                first, second = parts[low], parts[low | stride]
                parts[low], parts[low | stride] = first + second, first - second
        stride *= 2
    return parts


def local_kernel(scale, matrix_ref, signs_ref, hadamard_ref, out_ref, held):
    step = pl.program_id(0)
    blocks = held.shape[0]
    values = matrix_ref[...]
    flips = (2 * signs_ref[0] - 1).astype(jnp.float32)
    signed = (hadamard_ref[...].astype(jnp.float32) * flips).astype(jnp.bfloat16)
    high = values.astype(jnp.bfloat16)
    rest = values - high.astype(jnp.float32)
    middle = rest.astype(jnp.bfloat16)
    low = (rest - middle.astype(jnp.float32)).astype(jnp.bfloat16)
    total = jnp.dot(signed, low, preferred_element_type=jnp.float32)
    total += jnp.dot(signed, middle, preferred_element_type=jnp.float32)
    total += jnp.dot(signed, high, preferred_element_type=jnp.float32)
    held[step] = total * scale

    @pl.when(step == blocks - 1)
    def _():
        rows, width = held.shape[1], held.shape[2]

        def body(tile, carry):
            at = pl.multiple_of(tile * 8, 8)
            for column in range(0, width, 128):
                parts = [held[b, pl.ds(at, 8), column:column + 128] for b in range(blocks)]
                parts = butterflies(parts)
                for b in range(blocks):
                    out_ref[b, pl.ds(at, 8), column:column + 128] = parts[b]
            return carry

        lax.fori_loop(0, rows // 8, body, 0)


def local_mix(matrix_rows, signs, scale):
    length, width = matrix_rows.shape
    blocks = length // BLOCK
    hadamard = jnp.asarray(sylvester(BLOCK), jnp.bfloat16)
    out = pl.pallas_call(
        lambda *refs: local_kernel(scale, *refs),
        grid=(blocks,),
        out_shape=jax.ShapeDtypeStruct((blocks, BLOCK, width), jnp.float32),
        in_specs=[
            pl.BlockSpec((BLOCK, width), lambda b: (b, 0)),
            pl.BlockSpec((1, 1, BLOCK), lambda b: (b, 0, 0)),
            pl.BlockSpec((BLOCK, BLOCK), lambda b: (0, 0)),
        ],
        out_specs=pl.BlockSpec((blocks, BLOCK, width), lambda b: (0, 0, 0)),
        scratch_shapes=[pltpu.VMEM((blocks, BLOCK, width), jnp.float32)],
        compiler_params=pltpu.CompilerParams(vmem_limit_bytes=32 * 2**20),
        name="local_mix",
    )(matrix_rows, signs.reshape(blocks, 1, BLOCK), hadamard)
    return out


def across_kernel(in_ref, out_ref):
    count = in_ref.shape[0]
    inner = 8
    outer = count // inner
    for group in range(inner):
        parts = butterflies([in_ref[b * inner + group] for b in range(outer)])
        for b in range(outer):
            out_ref[b * inner + group] = parts[b]
    for group in range(outer):
        parts = butterflies([out_ref[group * inner + b] for b in range(inner)])
        for b in range(inner):
            out_ref[group * inner + b] = parts[b]


def across_mix(values):
    count, rows, width = values.shape
    spec = pl.BlockSpec((count, 8, 128), lambda r, c: (0, r, c))
    return pl.pallas_call(
        across_kernel,
        grid=(rows // 8, width // 128),
        out_shape=jax.ShapeDtypeStruct(values.shape, jnp.float32),
        in_specs=[spec],
        out_specs=spec,
        compiler_params=pltpu.CompilerParams(vmem_limit_bytes=32 * 2**20),
        name="across_mix",
    )(values)


def exchange(block):
    return lax.all_to_all(block, AXES, split_axis=0, concat_axis=0, tiled=True)


def on_device(matrix_rows, signs, picks):
    length, width = matrix_rows.shape
    owners = lax.axis_size("rows") * lax.axis_size("sub")
    share = length // owners
    scale = 1.0 / math.sqrt(length * owners)
    slots = picks[0]
    flat_picks = slots.reshape(-1)

    holder = (flat_picks // share)[:, None] == lax.broadcasted_iota(jnp.int32, (1, owners), 1)
    place = (flat_picks % share)[:, None] == lax.broadcasted_iota(jnp.int32, (1, share), 1)
    holder = holder & (flat_picks >= 0)[:, None]
    times = lax.dot_general(
        holder.astype(jnp.bfloat16), place.astype(jnp.bfloat16), (((0,), (0,)), ((), ())),
        preferred_element_type=jnp.float32,
    )
    times = exchange(times[:, None, :]).reshape(owners * share, 1)

    local = local_mix(matrix_rows, signs, scale)
    gathered = exchange(local.reshape(owners, share, width))
    whole = across_mix(gathered)
    values = exchange(whole).reshape(length, width)

    flat = whole.reshape(owners * share, width)
    gram = lax.dot_general(
        flat * times, flat, (((0,), (0,)), ((), ())),
        precision=lax.Precision.HIGHEST, preferred_element_type=jnp.float32,
    )
    gram = jnp.sum(exchange(gram.reshape(owners, width // owners, width)), axis=0)
    gram = exchange(jnp.broadcast_to(gram[None], (owners,) + gram.shape)).reshape(width, width)
    expected = owners * owners * slots.shape[1] / 2.0
    factor = jnp.linalg.cholesky(gram / expected).T

    taken = jnp.take(values, jnp.maximum(flat_picks, 0), axis=0)
    taken = jnp.where((flat_picks >= 0)[:, None], taken, jnp.float32(0.0))
    panel = exchange(taken.reshape(slots.shape[0], slots.shape[1], width)).reshape(-1, width)
    return (values, panel, factor)


def solution(mesh):
    placed = (P(AXES, None), P(AXES), P(AXES, None, None))
    return jax.shard_map(
        on_device,
        mesh=mesh,
        in_specs=placed,
        out_specs=(P(AXES, None), P(AXES, None), P()),
        check_vma=False,
    )
```

```python
import math

import jax
import jax.numpy as jnp
from jax import lax
from jax.experimental import pallas as pl
from jax.experimental.pallas import tpu as pltpu
from jax.sharding import PartitionSpec as P

AXES = ("rows", "sub")
TILE = 8
RADIX = 8
SUPER = 32
VMEM = 40 * 2**20
LARGE = 57 * 2**20


def butterflies(parts):
    count = len(parts)
    stride = 1
    while stride < count:
        for low in range(count):
            if low & stride == 0:
                first, second = parts[low], parts[low | stride]
                parts[low], parts[low | stride] = first + second, first - second
        stride *= 2
    return parts


def whole(space=pltpu.VMEM):
    return pl.BlockSpec(memory_space=space)


def local_kernel(scale, matrix_ref, signs_ref, out_ref, came, first, second, third, flips, signs_held, sems):
    halves, length, _ = came.shape
    share = out_ref.shape[1]
    size = length // RADIX
    group = TILE * RADIX
    loads = [
        [
            pltpu.make_async_copy(
                matrix_ref.at[pl.ds(c * size, size), h * 128:h * 128 + 128],
                came.at[h, pl.ds(c * size, size)],
                sems.at[c * halves + h],
            )
            for h in range(halves)
        ]
        for c in range(RADIX)
    ]
    signs_load = pltpu.make_async_copy(signs_ref, signs_held, sems.at[RADIX * halves])
    signs_load.start()
    for pair in loads:
        for load in pair:
            load.start()

    row = lax.broadcasted_iota(jnp.int32, (128, 128), 0)
    column = lax.broadcasted_iota(jnp.int32, (128, 128), 1)
    chosen = (row // 64 * 64 + row % 8 * 8 + row // 8 % 8 == column).astype(jnp.float32)
    ones = jnp.ones((128, 128), jnp.bfloat16)
    signs_load.wait()

    def flip(line, carry):
        signs = (2 * signs_held[pl.ds(line, 1), :] - 1).astype(jnp.float32)
        flips[pl.ds(pl.multiple_of(line * 128, 128), 128), :] = scale * jnp.dot(
            (chosen * signs).astype(jnp.bfloat16), ones, preferred_element_type=jnp.float32
        )
        return carry

    lax.fori_loop(0, length // 128, flip, 0, unroll=4)

    for c in range(RADIX):
        for load in loads[c]:
            load.wait()

        def inner(g, carry):
            base = pl.multiple_of(c * size + g * group, group)
            signs = [flips[pl.ds(base + TILE * s, TILE), :] for s in range(TILE)]
            for h in range(halves):
                parts = [came[h, pl.ds(base + s, RADIX, stride=TILE), :] * signs[s] for s in range(TILE)]
                parts = butterflies(parts)
                for s in range(TILE):
                    first[h, pl.ds(base + s, RADIX, stride=TILE), :] = parts[s]
            for h in range(halves):
                parts = butterflies([first[h, pl.ds(base + TILE * t, TILE), :] for t in range(RADIX)])
                for t in range(RADIX):
                    second[h, pl.ds(base + TILE * t, TILE), :] = parts[t]
            return carry

        lax.fori_loop(0, size // group, inner, 0, unroll=2)

        def outer(t, carry):
            base = pl.multiple_of(c * size + t * TILE, TILE)
            for h in range(halves):
                parts = butterflies([second[h, pl.ds(base + group * g, TILE), :] for g in range(size // group)])
                for g in range(size // group):
                    third[h, pl.ds(base + group * g, TILE), :] = parts[g]
            return carry

        lax.fori_loop(0, group // TILE, outer, 0, unroll=2)

    def last(q, carry):
        for t in range(share // TILE):
            for h in range(halves):
                at = pl.multiple_of(q * share, share) + t * TILE
                parts = butterflies([third[h, pl.ds(c * size + at, TILE), :] for c in range(RADIX)])
                for c in range(RADIX):
                    out_ref[c * (size // share) + q, t * TILE:(t + 1) * TILE, h * 128:h * 128 + 128] = parts[c]
        return carry

    lax.fori_loop(0, size // share, last, 0)


def local_mix(matrix_rows, signs, scale, owners):
    length, width = matrix_rows.shape
    halves = width // 128
    return pl.pallas_call(
        lambda *refs: local_kernel(scale, *refs),
        out_shape=jax.ShapeDtypeStruct((owners, length // owners, width), jnp.float32),
        in_specs=[whole(pltpu.HBM)] * 2,
        out_specs=whole(),
        scratch_shapes=[pltpu.VMEM((halves, length, 128), jnp.float32)] * 4
        + [
            pltpu.VMEM((length, 128), jnp.float32),
            pltpu.VMEM((length // 128, 128), jnp.int32),
            pltpu.SemaphoreType.DMA((RADIX * halves + 1,)),
        ],
        compiler_params=pltpu.CompilerParams(vmem_limit_bytes=LARGE),
        name="local_mix",
    )(matrix_rows, signs.reshape(length // 128, 128))


def across_kernel(in_ref, out_ref, held):
    count, rows, width = in_ref.shape
    inner = 8
    outer = count // inner

    def body(tile, carry):
        at = pl.multiple_of(tile * 8, 8)
        for half in range(width // 128):
            columns = slice(half * 128, half * 128 + 128)
            for group in range(inner):
                parts = butterflies([in_ref[b * inner + group, pl.ds(at, 8), columns] for b in range(outer)])
                for b in range(outer):
                    held[b * inner + group] = parts[b]
            for group in range(outer):
                parts = butterflies([held[group * inner + b] for b in range(inner)])
                for b in range(inner):
                    out_ref[group * inner + b, half, pl.ds(at, 8), :] = parts[b]
        return carry

    lax.fori_loop(0, rows // 8, body, 0)


def across_mix(values):
    count, rows, width = values.shape
    return pl.pallas_call(
        across_kernel,
        out_shape=jax.ShapeDtypeStruct((count, width // 128, rows, 128), jnp.float32),
        in_specs=[whole()],
        out_specs=whole(),
        scratch_shapes=[pltpu.VMEM((count, 8, 128), jnp.float32)],
        compiler_params=pltpu.CompilerParams(vmem_limit_bytes=VMEM),
        name="across_mix",
    )(values)


def pick_kernel(picks_ref, values_ref, mixed_ref, out_ref, taken, sems):
    halves, rows = values_ref.shape[1], values_ref.shape[2]
    tiles, _, slots, _ = taken.shape
    each = out_ref.shape[2]
    copies = [
        pltpu.make_async_copy(
            values_ref.at[:, half], mixed_ref.at[:, :, half * 128:half * 128 + 128], sems.at[half]
        )
        for half in range(halves)
    ]
    for copy in copies:
        copy.start()

    def body(tile, carry):
        for slot in range(slots):
            pick = picks_ref[slot % each, tile * (slots // each) + slot // each]
            row = jnp.maximum(pick, 0)
            for half in range(halves):
                part = values_ref[row // rows, half, pl.ds(row % rows, 1), :]
                taken[tile, half, slot:slot + 1, :] = jnp.where(pick >= 0, part, 0.0)
        for half in range(halves):
            for place in range(slots // each):
                out_ref[tile * (slots // each) + place, half] = (
                    taken[tile, half, place * each:(place + 1) * each, :]
                )
        return carry

    lax.fori_loop(0, tiles, body, 0, unroll=2)
    panel = jnp.concatenate([taken[:, half].reshape(-1, 128) for half in range(halves)], axis=1)
    gram = lax.dot_general(
        panel, panel, (((0,), (0,)), ((), ())),
        precision=lax.Precision.HIGHEST, preferred_element_type=jnp.float32,
    )
    each = gram.shape[0] // out_ref.shape[0]
    for owner in range(out_ref.shape[0]):
        for half in range(halves):
            out_ref[owner, halves, half * each:(half + 1) * each, :] = (
                gram[owner * each:(owner + 1) * each, half * 128:half * 128 + 128]
            )
    for copy in copies:
        copy.wait()


def pick_rows(values, picks):
    count, halves, rows, _ = values.shape
    slots, owners = picks.shape
    return pl.pallas_call(
        pick_kernel,
        out_shape=(
            jax.ShapeDtypeStruct((count, rows, halves * 128), jnp.float32),
            jax.ShapeDtypeStruct((owners, halves + 1, slots, 128), jnp.float32),
        ),
        in_specs=[whole(pltpu.SMEM), whole()],
        out_specs=(whole(pltpu.HBM), whole()),
        scratch_shapes=[
            pltpu.VMEM((slots * owners // TILE, halves, TILE, 128), jnp.float32),
            pltpu.SemaphoreType.DMA((halves,)),
        ],
        compiler_params=pltpu.CompilerParams(vmem_limit_bytes=VMEM),
        name="pick_rows",
    )(picks, values)


def sum_kernel(received_ref, out_ref):
    sources, last = received_ref.shape[0], received_ref.shape[1] - 1
    total = jnp.sum(received_ref[:, last], axis=0)
    out_ref[...] = jnp.broadcast_to(total[None], out_ref.shape)


def sum_pieces(received):
    sources, _, rows, width = received.shape
    return pl.pallas_call(
        sum_kernel,
        out_shape=jax.ShapeDtypeStruct((sources, rows, width), jnp.float32),
        in_specs=[whole()],
        out_specs=whole(),
        compiler_params=pltpu.CompilerParams(vmem_limit_bytes=VMEM),
        name="sum_pieces",
    )(received)


def panel_kernel(received_ref, panel_ref):
    sources, last, slots, _ = received_ref.shape
    for source in range(sources):
        for half in range(last - 1):
            panel_ref[source * slots:(source + 1) * slots, half * 128:half * 128 + 128] = (
                received_ref[source, half]
            )


def arrange_panel(received):
    sources, last, slots, width = received.shape
    return pl.pallas_call(
        panel_kernel,
        out_shape=jax.ShapeDtypeStruct((sources * slots, (last - 1) * width), jnp.float32),
        in_specs=[whole()],
        out_specs=whole(),
        compiler_params=pltpu.CompilerParams(vmem_limit_bytes=VMEM),
        name="arrange_panel",
    )(received)


def cholesky_kernel(expected, pieces_ref, out_ref, held):
    size = held.shape[0]
    halves = size // 128
    each = pieces_ref.shape[1] // halves
    for owner in range(pieces_ref.shape[0]):
        for half in range(halves):
            held[owner * each:(owner + 1) * each, half * 128:half * 128 + 128] = (
                pieces_ref[owner, half * each:(half + 1) * each, :] * (1.0 / expected)
            )
    place = lax.broadcasted_iota(jnp.int32, (TILE, 128), 0)
    lane = lax.broadcasted_iota(jnp.int32, (TILE, 128), 1)

    def spread_row(value, row):
        return jnp.broadcast_to(value[row:row + 1, :], (TILE, 128))

    def spread_column(value, column):
        return jnp.broadcast_to(value[:, column:column + 1], (TILE, 128))

    for base in range(0, size, SUPER):
        tiles = SUPER // TILE
        rows = [
            [held[base + t * TILE:base + (t + 1) * TILE, h * 128:h * 128 + 128] for h in range(halves)]
            for t in range(tiles)
        ]
        for t in range(tiles):
            first = base + t * TILE
            half, column = first // 128, first % 128
            edges = {
                u: [spread_column(rows[u][half], column + k) for k in range(TILE)]
                for u in range(t, tiles)
            }
            finished = list(rows[t])
            for k in range(TILE):
                pivot = spread_row(edges[t][k], k)
                inverse = 1.0 / pivot
                root = lax.rsqrt(pivot)
                root = root * (1.5 - 0.5 * pivot * root * root)
                lines = [spread_row(rows[t][h], k) for h in range(halves)]
                finished = [
                    jnp.where(place == k, lines[h] * root, finished[h]) for h in range(halves)
                ]
                lines = [line * inverse for line in lines]
                weights = [None] * TILE
                for m in range(k + 1, TILE):
                    weights[m] = spread_row(edges[t][k], m) * inverse
                for u in range(t, tiles):
                    edge = edges[u][k]
                    for m in range(k + 1, TILE):
                        edges[u][m] = edges[u][m] - edge * weights[m]
                    for h in range(halves):
                        rows[u][h] = rows[u][h] - edge * lines[h]
            rows[t] = [
                jnp.where(lane + h * 128 >= first + place, finished[h], 0.0) for h in range(halves)
            ]
            for h in range(halves):
                out_ref[first:first + TILE, h * 128:h * 128 + 128] = rows[t][h]
        after = base + SUPER
        if after < size:
            block = jnp.concatenate(
                [jnp.concatenate(rows[t], axis=1) for t in range(tiles)], axis=0
            )
            turned = block.T[after:]
            held[after:, :] -= jnp.dot(
                turned, block, precision=lax.Precision.HIGHEST, preferred_element_type=jnp.float32
            )


def upper_cholesky(pieces, expected):
    owners, rows, width = pieces.shape
    size = math.isqrt(owners * rows * width)
    return pl.pallas_call(
        lambda *refs: cholesky_kernel(expected, *refs),
        out_shape=jax.ShapeDtypeStruct((size, size), jnp.float32),
        in_specs=[whole()],
        out_specs=whole(),
        scratch_shapes=[pltpu.VMEM((size, size), jnp.float32)],
        compiler_params=pltpu.CompilerParams(vmem_limit_bytes=VMEM),
        name="upper_cholesky",
    )(pieces)


def exchange(block):
    return lax.all_to_all(block, AXES, split_axis=0, concat_axis=0, tiled=True)


def on_device(matrix_rows, signs, picks):
    length, width = matrix_rows.shape
    owners = lax.axis_size("rows") * lax.axis_size("sub")
    slots = picks.shape[2]
    scale = 1.0 / math.sqrt(length * owners)
    expected = owners * owners * slots / 2.0

    values = exchange(across_mix(exchange(local_mix(matrix_rows, signs, scale, owners))))
    mixed, taken = pick_rows(values, picks[0].T)
    received = exchange(taken)
    pieces = exchange(sum_pieces(received))
    factor = upper_cholesky(pieces, expected)
    panel = arrange_panel(received)
    return (mixed.reshape(length, width), panel, factor)


def solution(mesh):
    placed = (P(AXES, None), P(AXES), P(AXES, None, None))
    return jax.shard_map(
        on_device,
        mesh=mesh,
        in_specs=placed,
        out_specs=(P(AXES, None), P(AXES, None), P()),
        check_vma=False,
    )
```

```python
import math

import jax
import jax.numpy as jnp
from jax import lax
from jax.experimental import pallas as pl
from jax.experimental.pallas import tpu as pltpu
from jax.sharding import PartitionSpec as P

AXES = ("rows", "sub")
ROUND = ("sub", "rows")
TILE = 8
RADIX = 8
SUPER = 64
VMEM = 40 * 2**20
SMALL = 16 * 2**20
LARGE = 57 * 2**20


def butterflies(parts):
    count = len(parts)
    stride = 1
    while stride < count:
        for low in range(count):
            if low & stride == 0:
                first, second = parts[low], parts[low | stride]
                parts[low], parts[low | stride] = first + second, first - second
        stride *= 2
    return parts


def whole(space=pltpu.VMEM):
    return pl.BlockSpec(memory_space=space)


def local_kernel(scale, matrix_ref, signs_ref, out_ref, came, first, second, third, result, flips, signs_held, sems, out_sems):
    halves, length, _ = came.shape
    share = out_ref.shape[2]
    size = length // RADIX
    group = TILE * RADIX
    loads = [
        [
            pltpu.make_async_copy(
                matrix_ref.at[pl.ds(c * size, size), h * 128:h * 128 + 128],
                came.at[h, pl.ds(c * size, size)],
                sems.at[c * halves + h],
            )
            for h in range(halves)
        ]
        for c in range(RADIX)
    ]
    signs_load = pltpu.make_async_copy(signs_ref, signs_held, sems.at[RADIX * halves])
    signs_load.start()
    for pair in loads:
        for load in pair:
            load.start()

    row = lax.broadcasted_iota(jnp.int32, (128, 128), 0)
    column = lax.broadcasted_iota(jnp.int32, (128, 128), 1)
    chosen = (row // 64 * 64 + row % 8 * 8 + row // 8 % 8 == column).astype(jnp.float32)
    ones = jnp.ones((128, 128), jnp.bfloat16)
    signs_load.wait()

    def flip(line, carry):
        signs = (2 * signs_held[pl.ds(line, 1), :] - 1).astype(jnp.float32)
        flips[pl.ds(pl.multiple_of(line * 128, 128), 128), :] = scale * jnp.dot(
            (chosen * signs).astype(jnp.bfloat16), ones, preferred_element_type=jnp.float32
        )
        return carry

    lax.fori_loop(0, length // 128, flip, 0, unroll=4)

    for c in range(RADIX):
        for load in loads[c]:
            load.wait()

        def inner(g, carry):
            base = pl.multiple_of(c * size + g * group, group)
            signs = [flips[pl.ds(base + TILE * s, TILE), :] for s in range(TILE)]
            for h in range(halves):
                parts = [came[h, pl.ds(base + s, RADIX, stride=TILE), :] * signs[s] for s in range(TILE)]
                parts = butterflies(parts)
                for s in range(TILE):
                    first[h, pl.ds(base + s, RADIX, stride=TILE), :] = parts[s]
            for h in range(halves):
                parts = butterflies([first[h, pl.ds(base + TILE * t, TILE), :] for t in range(RADIX)])
                for t in range(RADIX):
                    second[h, pl.ds(base + TILE * t, TILE), :] = parts[t]
            return carry

        lax.fori_loop(0, size // group, inner, 0, unroll=2)

        def outer(t, carry):
            base = pl.multiple_of(c * size + t * TILE, TILE)
            for h in range(halves):
                parts = butterflies([second[h, pl.ds(base + group * g, TILE), :] for g in range(size // group)])
                for g in range(size // group):
                    third[h, pl.ds(base + group * g, TILE), :] = parts[g]
            return carry

        lax.fori_loop(0, group // TILE, outer, 0, unroll=2)

    def send(q):
        return pltpu.make_async_copy(result.at[:, q], out_ref.at[:, q], out_sems.at[q])

    def last(q, carry):
        for t in range(share // TILE):
            for h in range(halves):
                at = pl.multiple_of(q * share, share) + t * TILE
                parts = butterflies([third[h, pl.ds(c * size + at, TILE), :] for c in range(RADIX)])
                for c in range(RADIX):
                    result[c, q, t * TILE:(t + 1) * TILE, h * 128:h * 128 + 128] = parts[c]
        send(q).start()
        return carry

    lax.fori_loop(0, size // share, last, 0)
    for q in range(size // share):
        send(q).wait()


def local_mix(matrix_rows, signs, scale, owners):
    length, width = matrix_rows.shape
    halves = width // 128
    shape = (RADIX, owners // RADIX, length // owners, width)
    mixed = pl.pallas_call(
        lambda *refs: local_kernel(scale, *refs),
        out_shape=jax.ShapeDtypeStruct(shape, jnp.float32),
        in_specs=[whole(pltpu.HBM)] * 2,
        out_specs=whole(pltpu.HBM),
        scratch_shapes=[pltpu.VMEM((halves, length, 128), jnp.float32)] * 4
        + [
            pltpu.VMEM(shape, jnp.float32),
            pltpu.VMEM((length, 128), jnp.float32),
            pltpu.VMEM((length // 128, 128), jnp.int32),
            pltpu.SemaphoreType.DMA((RADIX * halves + 1,)),
            pltpu.SemaphoreType.DMA((owners // RADIX,)),
        ],
        compiler_params=pltpu.CompilerParams(vmem_limit_bytes=LARGE),
        name="local_mix",
    )(matrix_rows, signs.reshape(length // 128, 128))
    return mixed.reshape(owners, length // owners, width)


def across_kernel(in_ref, out_ref, held):
    count, rows, width = in_ref.shape
    inner = 8
    outer = count // inner

    def body(tile, carry):
        at = pl.multiple_of(tile * 8, 8)
        for half in range(width // 128):
            columns = slice(half * 128, half * 128 + 128)
            for group in range(inner):
                parts = butterflies([in_ref[b * inner + group, pl.ds(at, 8), columns] for b in range(outer)])
                for b in range(outer):
                    held[b * inner + group] = parts[b]
            for group in range(outer):
                parts = butterflies([held[group * inner + b] for b in range(inner)])
                for b in range(inner):
                    out_ref[group * inner + b, half, pl.ds(at, 8), :] = parts[b]
        return carry

    lax.fori_loop(0, rows // 8, body, 0)


def across_mix(values):
    count, rows, width = values.shape
    return pl.pallas_call(
        across_kernel,
        out_shape=jax.ShapeDtypeStruct((count, width // 128, rows, 128), jnp.float32),
        in_specs=[whole()],
        out_specs=whole(),
        scratch_shapes=[pltpu.VMEM((count, 8, 128), jnp.float32)],
        compiler_params=pltpu.CompilerParams(vmem_limit_bytes=VMEM),
        name="across_mix",
    )(values)


def turn(device, count):
    return device % 2 * (count // 2) + device // 2


def split(values):
    high = values.astype(jnp.bfloat16)
    rest = values - high.astype(jnp.float32)
    middle = rest.astype(jnp.bfloat16)
    low = (rest - middle.astype(jnp.float32)).astype(jnp.bfloat16)
    return high, middle, low


def square(block):
    high, middle, low = split(block.T)
    left = jnp.concatenate([high, low, middle, high, middle, high], axis=1)
    high, middle, low = split(block)
    right = jnp.concatenate([low, high, middle, middle, high, high], axis=0)
    return left, right


def pick_kernel(picks_ref, values_ref, out_ref, taken):
    count, halves, rows, width = values_ref.shape
    tiles, _, slots, _ = taken.shape
    owners, _, each, _ = out_ref.shape
    shift = rows.bit_length() - 1
    flat = values_ref.reshape(count * halves * rows, width)

    def body(tile, carry):
        for slot in range(slots):
            pair, place = slot // each, slot % each
            pick = picks_ref[place, tile * 2 + pair]
            row = jnp.maximum(pick, 0)
            at = (row >> shift) * (halves * rows) + (row & (rows - 1))
            for half in range(halves):
                part = jnp.where(pick >= 0, flat[pl.ds(at + half * rows, 1), :], 0.0)
                taken[tile, half, slot:slot + 1, :] = part
                out_ref[pair * (owners // 2) + tile, half, place:place + 1, :] = part
        return carry

    lax.fori_loop(0, tiles, body, 0, unroll=4)
    panel = jnp.concatenate([taken[:, half].reshape(-1, 128) for half in range(halves)], axis=1)
    left, right = square(panel)
    gram = jnp.dot(left, right, preferred_element_type=jnp.float32)
    each = gram.shape[0] // out_ref.shape[0]
    for owner in range(out_ref.shape[0]):
        for half in range(halves):
            out_ref[owner, halves, half * each:(half + 1) * each, :] = (
                gram[owner * each:(owner + 1) * each, half * 128:half * 128 + 128]
            )


def pick_rows(values, picks):
    halves = values.shape[1]
    slots, owners = picks.shape
    return pl.pallas_call(
        pick_kernel,
        out_shape=jax.ShapeDtypeStruct((owners, halves + 1, slots, 128), jnp.float32),
        in_specs=[whole(pltpu.SMEM), whole()],
        out_specs=whole(),
        scratch_shapes=[pltpu.VMEM((slots * owners // TILE, halves, TILE, 128), jnp.float32)],
        compiler_params=pltpu.CompilerParams(vmem_limit_bytes=SMALL),
        name="pick_rows",
    )(picks, values)


def sum_kernel(received_ref, out_ref):
    sources, last = received_ref.shape[0], received_ref.shape[1] - 1
    total = jnp.sum(received_ref[:, last], axis=0)
    out_ref[...] = jnp.broadcast_to(total[None], out_ref.shape)


def sum_pieces(received):
    sources, _, rows, width = received.shape
    return pl.pallas_call(
        sum_kernel,
        out_shape=jax.ShapeDtypeStruct((sources, rows, width), jnp.float32),
        in_specs=[whole()],
        out_specs=whole(),
        compiler_params=pltpu.CompilerParams(vmem_limit_bytes=VMEM),
        name="sum_pieces",
    )(received)


def finish_kernel(expected, pieces_ref, received_ref, values_ref, mixed_ref, panel_ref, out_ref, held, panel, sems):
    size = held.shape[0]
    halves = size // 128
    copies = [
        pltpu.make_async_copy(
            values_ref.at[:, half], mixed_ref.at[:, :, half * 128:half * 128 + 128], sems.at[half]
        )
        for half in range(halves)
    ]
    copies.append(pltpu.make_async_copy(panel, panel_ref, sems.at[halves]))
    for copy in copies[:halves]:
        copy.start()
    sources, _, slots, _ = received_ref.shape
    for source in range(sources):
        for half in range(halves):
            panel[source * slots:(source + 1) * slots, half * 128:half * 128 + 128] = (
                received_ref[turn(source, sources), half]
            )
    copies[halves].start()
    each = pieces_ref.shape[1] // halves
    for owner in range(pieces_ref.shape[0]):
        for half in range(halves):
            held[owner * each:(owner + 1) * each, half * 128:half * 128 + 128] = (
                pieces_ref[owner, half * each:(half + 1) * each, :] * (1.0 / expected)
            )
    place = lax.broadcasted_iota(jnp.int32, (TILE, 128), 0)
    lane = lax.broadcasted_iota(jnp.int32, (TILE, 128), 1)

    def spread_row(value, row):
        return jnp.broadcast_to(value[row:row + 1, :], (TILE, 128))

    def spread_column(value, column):
        return jnp.broadcast_to(value[:, column:column + 1], (TILE, 128))

    for base in range(0, size, SUPER):
        tiles = SUPER // TILE
        rows = [
            [held[base + t * TILE:base + (t + 1) * TILE, h * 128:h * 128 + 128] for h in range(halves)]
            for t in range(tiles)
        ]
        for t in range(tiles):
            first = base + t * TILE
            half, column = first // 128, first % 128
            edges = {
                u: [spread_column(rows[u][half], column + k) for k in range(TILE)]
                for u in range(t, tiles)
            }
            finished = list(rows[t])
            for k in range(TILE):
                pivot = spread_row(edges[t][k], k)
                inverse = 1.0 / pivot
                root = lax.rsqrt(pivot)
                root = root * (1.5 - 0.5 * pivot * root * root)
                lines = [spread_row(rows[t][h], k) for h in range(halves)]
                finished = [
                    jnp.where(place == k, lines[h] * root, finished[h]) for h in range(halves)
                ]
                lines = [line * inverse for line in lines]
                weights = [None] * TILE
                for m in range(k + 1, TILE):
                    weights[m] = spread_row(edges[t][k], m) * inverse
                for u in range(t, tiles):
                    edge = edges[u][k]
                    for m in range(k + 1, TILE):
                        edges[u][m] = edges[u][m] - edge * weights[m]
                    for h in range(halves):
                        rows[u][h] = rows[u][h] - edge * lines[h]
            rows[t] = [
                jnp.where(lane + h * 128 >= first + place, finished[h], 0.0) for h in range(halves)
            ]
            for h in range(halves):
                out_ref[first:first + TILE, h * 128:h * 128 + 128] = rows[t][h]
        after = base + SUPER
        if after < size:
            block = jnp.concatenate(
                [jnp.concatenate(rows[t], axis=1) for t in range(tiles)], axis=0
            )
            left, right = square(block)
            held[after:, :] -= jnp.dot(left[after:], right, preferred_element_type=jnp.float32)
    for copy in copies:
        copy.wait()


def finish(pieces, received, values, expected):
    owners, rows, width = pieces.shape
    count, halves, share, _ = values.shape
    size = halves * width
    panel = jax.ShapeDtypeStruct((received.shape[0] * received.shape[2], size), jnp.float32)
    return pl.pallas_call(
        lambda *refs: finish_kernel(expected, *refs),
        out_shape=(
            jax.ShapeDtypeStruct((count, share, size), jnp.float32),
            panel,
            jax.ShapeDtypeStruct((size, size), jnp.float32),
        ),
        in_specs=[whole()] * 3,
        out_specs=(whole(pltpu.HBM), whole(pltpu.HBM), whole()),
        scratch_shapes=[
            pltpu.VMEM((size, size), jnp.float32),
            pltpu.VMEM(panel.shape, jnp.float32),
            pltpu.SemaphoreType.DMA((halves + 1,)),
        ],
        compiler_params=pltpu.CompilerParams(vmem_limit_bytes=SMALL),
        name="finish",
    )(pieces, received, values)


def exchange(block):
    return lax.all_to_all(block, ROUND, split_axis=0, concat_axis=0, tiled=True)


def on_device(matrix_rows, signs, picks):
    length, width = matrix_rows.shape
    owners = lax.axis_size("rows") * lax.axis_size("sub")
    slots = picks.shape[2]
    scale = 1.0 / math.sqrt(length * owners)
    expected = owners * owners * slots / 2.0

    values = exchange(across_mix(exchange(local_mix(matrix_rows, signs, scale, owners))))
    received = exchange(pick_rows(values, picks[0].T))
    pieces = exchange(sum_pieces(received))
    mixed, panel, factor = finish(pieces, received, values, expected)
    return (mixed.reshape(length, width), panel, factor)


def solution(mesh):
    placed = (P(AXES, None), P(AXES), P(AXES, None, None))
    return jax.shard_map(
        on_device,
        mesh=mesh,
        in_specs=placed,
        out_specs=(P(AXES, None), P(AXES, None), P()),
        check_vma=False,
    )
```

```python
import math

import jax
import jax.numpy as jnp
from jax import lax
from jax.experimental import pallas as pl
from jax.experimental.pallas import tpu as pltpu
from jax.sharding import Mesh, PartitionSpec as P

AXES = ("y_low", "x", "z", "core", "y_high")
SIZES = (2, 4, 4, 2, 2)
ROUND = ("z", "y_high", "y_low", "x", "core")
TILE = 8
RADIX = 8
AT_ONCE = 16
SUPER = 64
VMEM = 40 * 2**20
SMALL = 16 * 2**20
LARGE = 57 * 2**20


def butterflies(parts):
    count = len(parts)
    stride = 1
    while stride < count:
        for low in range(count):
            if low & stride == 0:
                first, second = parts[low], parts[low | stride]
                parts[low], parts[low | stride] = first + second, first - second
        stride *= 2
    return parts


def whole(space=pltpu.VMEM):
    return pl.BlockSpec(memory_space=space)


def local_kernel(scale, matrix_ref, signs_ref, out_ref, came, first, second, third, result, flips, signs_held, sems, out_sems):
    halves, length, _ = came.shape
    share = out_ref.shape[2]
    size = length // RADIX
    group = TILE * RADIX
    loads = [
        [
            pltpu.make_async_copy(
                matrix_ref.at[pl.ds(c * size, size), h * 128:h * 128 + 128],
                came.at[h, pl.ds(c * size, size)],
                sems.at[c * halves + h],
            )
            for h in range(halves)
        ]
        for c in range(RADIX)
    ]
    signs_load = pltpu.make_async_copy(signs_ref, signs_held, sems.at[RADIX * halves])
    signs_load.start()
    for pair in loads:
        for load in pair:
            load.start()

    row = lax.broadcasted_iota(jnp.int32, (128, 128), 0)
    column = lax.broadcasted_iota(jnp.int32, (128, 128), 1)
    chosen = (row // 64 * 64 + row % 8 * 8 + row // 8 % 8 == column).astype(jnp.float32)
    ones = jnp.ones((128, 128), jnp.bfloat16)
    signs_load.wait()

    def flip(line, carry):
        signs = (2 * signs_held[pl.ds(line, 1), :] - 1).astype(jnp.float32)
        flips[pl.ds(pl.multiple_of(line * 128, 128), 128), :] = scale * jnp.dot(
            (chosen * signs).astype(jnp.bfloat16), ones, preferred_element_type=jnp.float32
        )
        return carry

    lax.fori_loop(0, length // 128, flip, 0, unroll=16)

    for c in range(RADIX):
        for load in loads[c]:
            load.wait()

        def inner(g, carry):
            base = pl.multiple_of(c * size + g * group, group)
            signs = [flips[pl.ds(base + TILE * s, TILE), :] for s in range(TILE)]
            for h in range(halves):
                parts = [came[h, pl.ds(base + s, RADIX, stride=TILE), :] * signs[s] for s in range(TILE)]
                parts = butterflies(parts)
                for s in range(TILE):
                    first[h, pl.ds(base + s, RADIX, stride=TILE), :] = parts[s]
            for h in range(halves):
                parts = butterflies([first[h, pl.ds(base + TILE * t, TILE), :] for t in range(RADIX)])
                for t in range(RADIX):
                    second[h, pl.ds(base + TILE * t, TILE), :] = parts[t]
            return carry

        lax.fori_loop(0, size // group, inner, 0, unroll=8)

        def outer(t, carry):
            base = pl.multiple_of(c * size + t * TILE, TILE)
            for h in range(halves):
                parts = butterflies([second[h, pl.ds(base + group * g, TILE), :] for g in range(size // group)])
                for g in range(size // group):
                    third[h, pl.ds(base + group * g, TILE), :] = parts[g]
            return carry

        lax.fori_loop(0, group // TILE, outer, 0, unroll=8)

    def send(q):
        return pltpu.make_async_copy(result.at[:, q], out_ref.at[:, q], out_sems.at[q])

    def last(q, carry):
        for t in range(share // TILE):
            for h in range(halves):
                at = pl.multiple_of(q * share, share) + t * TILE
                parts = butterflies([third[h, pl.ds(c * size + at, TILE), :] for c in range(RADIX)])
                for c in range(RADIX):
                    result[c, q, t * TILE:(t + 1) * TILE, h * 128:h * 128 + 128] = parts[c]
        send(q).start()
        return carry

    lax.fori_loop(0, size // share, last, 0, unroll=2)
    for q in range(size // share):
        send(q).wait()


def local_mix(matrix_rows, signs, scale, owners):
    length, width = matrix_rows.shape
    halves = width // 128
    shape = (RADIX, owners // RADIX, length // owners, width)
    mixed = pl.pallas_call(
        lambda *refs: local_kernel(scale, *refs),
        out_shape=jax.ShapeDtypeStruct(shape, jnp.float32),
        in_specs=[whole(pltpu.HBM)] * 2,
        out_specs=whole(pltpu.HBM),
        scratch_shapes=[pltpu.VMEM((halves, length, 128), jnp.float32)] * 4
        + [
            pltpu.VMEM(shape, jnp.float32),
            pltpu.VMEM((length, 128), jnp.float32),
            pltpu.VMEM((length // 128, 128), jnp.int32),
            pltpu.SemaphoreType.DMA((RADIX * halves + 1,)),
            pltpu.SemaphoreType.DMA((owners // RADIX,)),
        ],
        compiler_params=pltpu.CompilerParams(vmem_limit_bytes=LARGE),
        name="local_mix",
    )(matrix_rows, signs.reshape(length // 128, 128))
    return mixed.reshape(owners, length // owners, width)


def across_kernel(in_ref, out_ref, held):
    count, rows, width = in_ref.shape
    inner = 8
    outer = count // inner

    def body(tile, carry):
        at = pl.multiple_of(tile * 8, 8)
        for half in range(width // 128):
            columns = slice(half * 128, half * 128 + 128)
            for group in range(inner):
                parts = butterflies([in_ref[b * inner + group, pl.ds(at, 8), columns] for b in range(outer)])
                for b in range(outer):
                    held[b * inner + group] = parts[b]
            for group in range(outer):
                parts = butterflies([held[group * inner + b] for b in range(inner)])
                for b in range(inner):
                    out_ref[group * inner + b, half, pl.ds(at, 8), :] = parts[b]
        return carry

    lax.fori_loop(0, rows // 8, body, 0)


def across_mix(values):
    count, rows, width = values.shape
    return pl.pallas_call(
        across_kernel,
        out_shape=jax.ShapeDtypeStruct((count, width // 128, rows, 128), jnp.float32),
        in_specs=[whole()],
        out_specs=whole(),
        scratch_shapes=[pltpu.VMEM((count, 8, 128), jnp.float32)],
        compiler_params=pltpu.CompilerParams(vmem_limit_bytes=VMEM),
        name="across_mix",
    )(values)


def turn(device):
    weights, weight = {}, 1
    for axis in reversed(ROUND):
        weights[axis] = weight
        weight *= SIZES[AXES.index(axis)]
    place = 0
    for axis, size in zip(reversed(AXES), reversed(SIZES)):
        place = place + (device & (size - 1)) * weights[axis]
        device = device >> (size.bit_length() - 1)
    return place


def split(values):
    high = values.astype(jnp.bfloat16)
    rest = values - high.astype(jnp.float32)
    middle = rest.astype(jnp.bfloat16)
    low = (rest - middle.astype(jnp.float32)).astype(jnp.bfloat16)
    return high, middle, low


def factors(parts, others, axis):
    high, middle, low = parts
    left = jnp.concatenate([high, low, middle, high, middle, high], axis=axis)
    high, middle, low = others
    right = jnp.concatenate([low, high, middle, middle, high, high], axis=0)
    return left, right


def pick_kernel(picks_ref, values_ref, out_ref, taken):
    count, halves, rows, width = values_ref.shape
    tiles, _, slots, _ = taken.shape
    owners, _, each, _ = out_ref.shape
    shift = rows.bit_length() - 1
    flat = values_ref.reshape(count * halves * rows, width)

    def body(step, carry):
        first = turn(step * (2 * AT_ONCE))
        for number in range(AT_ONCE):
            tile = step * AT_ONCE + number
            for slot in range(slots):
                pair, place = number * 2 + slot // each, slot % each
                pick = picks_ref[place, step * (2 * AT_ONCE) + pair]
                row = jnp.maximum(pick, 0)
                at = (row >> shift) * (halves * rows) + (row & (rows - 1))
                for half in range(halves):
                    part = jnp.where(pick >= 0, flat[pl.ds(at + half * rows, 1), :], 0.0)
                    taken[tile, half, slot:slot + 1, :] = part
                    out_ref[first + turn(pair), half, place:place + 1, :] = part
        return carry

    lax.fori_loop(0, tiles // AT_ONCE, body, 0)
    panel = jnp.concatenate([taken[:, half].reshape(-1, 128) for half in range(halves)], axis=1)
    left, right = factors(split(panel.T), split(panel), 1)
    gram = jnp.dot(left, right, preferred_element_type=jnp.float32)
    each = gram.shape[0] // out_ref.shape[0]
    for owner in range(out_ref.shape[0]):
        for half in range(halves):
            out_ref[owner, halves, half * each:(half + 1) * each, :] = (
                gram[owner * each:(owner + 1) * each, half * 128:half * 128 + 128]
            )


def pick_rows(values, picks):
    halves = values.shape[1]
    slots, owners = picks.shape
    return pl.pallas_call(
        pick_kernel,
        out_shape=jax.ShapeDtypeStruct((owners, halves + 1, slots, 128), jnp.float32),
        in_specs=[whole(pltpu.SMEM), whole()],
        out_specs=whole(),
        scratch_shapes=[pltpu.VMEM((slots * owners // TILE, halves, TILE, 128), jnp.float32)],
        compiler_params=pltpu.CompilerParams(vmem_limit_bytes=SMALL),
        name="pick_rows",
    )(picks, values)


def finish_kernel(expected, pieces_ref, received_ref, values_ref, mixed_ref, panel_ref, out_ref, held, panel, sems):
    size = held.shape[0]
    halves = size // 128
    copies = [
        pltpu.make_async_copy(
            values_ref.at[:, half], mixed_ref.at[:, :, half * 128:half * 128 + 128], sems.at[half]
        )
        for half in range(halves)
    ]
    copies.append(pltpu.make_async_copy(panel, panel_ref, sems.at[halves]))
    for copy in copies[:halves]:
        copy.start()
    sources, _, slots, _ = received_ref.shape
    for source in range(sources):
        for half in range(halves):
            panel[source * slots:(source + 1) * slots, half * 128:half * 128 + 128] = (
                received_ref[turn(source), half]
            )
    copies[halves].start()
    each = pieces_ref.shape[1] // halves
    for owner in range(pieces_ref.shape[0]):
        for half in range(halves):
            held[owner * each:(owner + 1) * each, half * 128:half * 128 + 128] = (
                pieces_ref[owner, half * each:(half + 1) * each, :] * (1.0 / expected)
            )
    place = lax.broadcasted_iota(jnp.int32, (TILE, 128), 0)
    lane = lax.broadcasted_iota(jnp.int32, (TILE, 128), 1)

    def spread_row(value, row):
        return jnp.broadcast_to(value[row:row + 1, :], (TILE, 128))

    def spread_column(value, column):
        return jnp.broadcast_to(value[:, column:column + 1], (TILE, 128))

    for base in range(0, size, SUPER):
        tiles = SUPER // TILE
        rows = [
            [held[base + t * TILE:base + (t + 1) * TILE, h * 128:h * 128 + 128] for h in range(halves)]
            for t in range(tiles)
        ]
        for t in range(tiles):
            first = base + t * TILE
            half, column = first // 128, first % 128
            edges = {
                u: [spread_column(rows[u][half], column + k) for k in range(TILE)]
                for u in range(t, tiles)
            }
            finished = list(rows[t])
            for k in range(TILE):
                pivot = spread_row(edges[t][k], k)
                inverse = 1.0 / pivot
                root = lax.rsqrt(pivot)
                root = root * (1.5 - 0.5 * pivot * root * root)
                lines = [spread_row(rows[t][h], k) for h in range(halves)]
                finished = [
                    jnp.where(place == k, lines[h] * root, finished[h]) for h in range(halves)
                ]
                lines = [line * inverse for line in lines]
                weights = [None] * TILE
                for m in range(k + 1, TILE):
                    weights[m] = spread_row(edges[t][k], m) * inverse
                for u in range(t, tiles):
                    edge = edges[u][k]
                    for m in range(k + 1, TILE):
                        edges[u][m] = edges[u][m] - edge * weights[m]
                    for h in range(halves):
                        rows[u][h] = rows[u][h] - edge * lines[h]
            rows[t] = [
                jnp.where(lane + h * 128 >= first + place, finished[h], 0.0) for h in range(halves)
            ]
            for h in range(halves):
                out_ref[first:first + TILE, h * 128:h * 128 + 128] = rows[t][h]
        after = base + SUPER
        if after < size:
            block = jnp.concatenate(
                [jnp.concatenate(rows[t], axis=1) for t in range(tiles)], axis=0
            )
            left, right = factors(split(block), split(block), 0)
            held[after:, :] -= jnp.dot(left.T[after:], right, preferred_element_type=jnp.float32)
    for copy in copies:
        copy.wait()


def finish(pieces, received, values, expected):
    owners, rows, width = pieces.shape
    count, halves, share, _ = values.shape
    size = halves * width
    panel = jax.ShapeDtypeStruct((received.shape[0] * received.shape[2], size), jnp.float32)
    return pl.pallas_call(
        lambda *refs: finish_kernel(expected, *refs),
        out_shape=(
            jax.ShapeDtypeStruct((count, share, size), jnp.float32),
            panel,
            jax.ShapeDtypeStruct((size, size), jnp.float32),
        ),
        in_specs=[whole()] * 3,
        out_specs=(whole(pltpu.HBM), whole(pltpu.HBM), whole()),
        scratch_shapes=[
            pltpu.VMEM((size, size), jnp.float32),
            pltpu.VMEM(panel.shape, jnp.float32),
            pltpu.SemaphoreType.DMA((halves + 1,)),
        ],
        compiler_params=pltpu.CompilerParams(vmem_limit_bytes=SMALL),
        name="finish",
    )(pieces, received, values)


def exchange(block):
    return lax.all_to_all(block, ROUND, split_axis=0, concat_axis=0, tiled=True)


def on_device(matrix_rows, signs, picks):
    length, width = matrix_rows.shape
    owners = math.prod(SIZES)
    slots = picks.shape[2]
    scale = 1.0 / math.sqrt(length * owners)
    expected = owners * owners * slots / 2.0

    values = exchange(across_mix(exchange(local_mix(matrix_rows, signs, scale, owners))))
    received = exchange(pick_rows(values, picks[0].T))
    piece = jnp.sum(received[:, -1], axis=0)
    pieces = exchange(jnp.broadcast_to(piece, (owners,) + piece.shape))
    mixed, panel, factor = finish(pieces, received, values, expected)
    return (mixed.reshape(length, width), panel, factor)


def solution(mesh):
    placed = (P(AXES, None), P(AXES), P(AXES, None, None))
    return jax.shard_map(
        on_device,
        mesh=Mesh(mesh.devices.reshape(SIZES), AXES),
        in_specs=placed,
        out_specs=(P(AXES, None), P(AXES, None), P()),
        check_vma=False,
    )
```

```python
import math

import jax
import jax.numpy as jnp
from jax import lax
from jax.experimental import pallas as pl
from jax.experimental.pallas import tpu as pltpu
from jax.sharding import Mesh, PartitionSpec as P

AXES = ("y_low", "x", "z", "core", "y_high")
SIZES = (2, 4, 4, 2, 2)
ROUND = ("z", "core", "x", "y_high", "y_low")
TILE = 8
RADIX = 8
AT_ONCE = 16
MOVES = 4
SUPER = 64
VMEM = 40 * 2**20
SMALL = 16 * 2**20
LARGE = 57 * 2**20


def butterflies(parts):
    count = len(parts)
    stride = 1
    while stride < count:
        for low in range(count):
            if low & stride == 0:
                first, second = parts[low], parts[low | stride]
                parts[low], parts[low | stride] = first + second, first - second
        stride *= 2
    return parts


def whole(space=pltpu.VMEM):
    return pl.BlockSpec(memory_space=space)


def local_kernel(scale, matrix_ref, signs_ref, out_ref, came, first, second, third, result, flips, signs_held, sems, out_sems):
    halves, length, _ = came.shape
    share = out_ref.shape[2]
    size = length // RADIX
    group = TILE * RADIX
    loads = [
        [
            pltpu.make_async_copy(
                matrix_ref.at[pl.ds(c * size, size), h * 128:h * 128 + 128],
                came.at[h, pl.ds(c * size, size)],
                sems.at[c * halves + h],
            )
            for h in range(halves)
        ]
        for c in range(RADIX)
    ]
    signs_load = pltpu.make_async_copy(signs_ref, signs_held, sems.at[RADIX * halves])
    signs_load.start()
    for pair in loads:
        for load in pair:
            load.start()

    row = lax.broadcasted_iota(jnp.int32, (128, 128), 0)
    column = lax.broadcasted_iota(jnp.int32, (128, 128), 1)
    chosen = (row // 64 * 64 + row % 8 * 8 + row // 8 % 8 == column).astype(jnp.float32)
    ones = jnp.ones((128, 128), jnp.bfloat16)
    signs_load.wait()

    def flip(line, carry):
        signs = (2 * signs_held[pl.ds(line, 1), :] - 1).astype(jnp.float32)
        flips[pl.ds(pl.multiple_of(line * 128, 128), 128), :] = scale * jnp.dot(
            (chosen * signs).astype(jnp.bfloat16), ones, preferred_element_type=jnp.float32
        )
        return carry

    lax.fori_loop(0, length // 128, flip, 0, unroll=16)

    for c in range(RADIX):
        for load in loads[c]:
            load.wait()

        def inner(g, carry):
            base = pl.multiple_of(c * size + g * group, group)
            signs = [flips[pl.ds(base + TILE * s, TILE), :] for s in range(TILE)]
            for h in range(halves):
                parts = [came[h, pl.ds(base + s, RADIX, stride=TILE), :] * signs[s] for s in range(TILE)]
                parts = butterflies(parts)
                for s in range(TILE):
                    first[h, pl.ds(base + s, RADIX, stride=TILE), :] = parts[s]
            for h in range(halves):
                parts = butterflies([first[h, pl.ds(base + TILE * t, TILE), :] for t in range(RADIX)])
                for t in range(RADIX):
                    second[h, pl.ds(base + TILE * t, TILE), :] = parts[t]
            return carry

        lax.fori_loop(0, size // group, inner, 0, unroll=8)

        def outer(t, carry):
            base = pl.multiple_of(c * size + t * TILE, TILE)
            for h in range(halves):
                parts = butterflies([second[h, pl.ds(base + group * g, TILE), :] for g in range(size // group)])
                for g in range(size // group):
                    third[h, pl.ds(base + group * g, TILE), :] = parts[g]
            return carry

        lax.fori_loop(0, group // TILE, outer, 0, unroll=8)

    def send(q):
        return pltpu.make_async_copy(result.at[:, q], out_ref.at[:, q], out_sems.at[q])

    def last(q, carry):
        for t in range(share // TILE):
            for h in range(halves):
                at = pl.multiple_of(q * share, share) + t * TILE
                parts = butterflies([third[h, pl.ds(c * size + at, TILE), :] for c in range(RADIX)])
                for c in range(RADIX):
                    result[c, q, t * TILE:(t + 1) * TILE, h * 128:h * 128 + 128] = parts[c]
        send(q).start()
        return carry

    lax.fori_loop(0, size // share, last, 0, unroll=2)
    for q in range(size // share):
        send(q).wait()


def local_mix(matrix_rows, signs, scale, owners):
    length, width = matrix_rows.shape
    halves = width // 128
    shape = (RADIX, owners // RADIX, length // owners, width)
    mixed = pl.pallas_call(
        lambda *refs: local_kernel(scale, *refs),
        out_shape=jax.ShapeDtypeStruct(shape, jnp.float32),
        in_specs=[whole(pltpu.HBM)] * 2,
        out_specs=whole(pltpu.HBM),
        scratch_shapes=[pltpu.VMEM((halves, length, 128), jnp.float32)] * 4
        + [
            pltpu.VMEM(shape, jnp.float32),
            pltpu.VMEM((length, 128), jnp.float32),
            pltpu.VMEM((length // 128, 128), jnp.int32),
            pltpu.SemaphoreType.DMA((RADIX * halves + 1,)),
            pltpu.SemaphoreType.DMA((owners // RADIX,)),
        ],
        compiler_params=pltpu.CompilerParams(vmem_limit_bytes=LARGE),
        name="local_mix",
    )(matrix_rows, signs.reshape(length // 128, 128))
    return mixed.reshape(owners, length // owners, width)


def across_kernel(in_ref, out_ref, held):
    count, rows, width = in_ref.shape
    inner = 8
    outer = count // inner

    def body(tile, carry):
        at = pl.multiple_of(tile * 8, 8)
        for half in range(width // 128):
            columns = slice(half * 128, half * 128 + 128)
            for group in range(inner):
                parts = butterflies([in_ref[b * inner + group, pl.ds(at, 8), columns] for b in range(outer)])
                for b in range(outer):
                    held[b * inner + group] = parts[b]
            for group in range(outer):
                parts = butterflies([held[group * inner + b] for b in range(inner)])
                for b in range(inner):
                    out_ref[group * inner + b, half, pl.ds(at, 8), :] = parts[b]
        return carry

    lax.fori_loop(0, rows // 8, body, 0)


def across_mix(values):
    count, rows, width = values.shape
    return pl.pallas_call(
        across_kernel,
        out_shape=jax.ShapeDtypeStruct((count, width // 128, rows, 128), jnp.float32),
        in_specs=[whole()],
        out_specs=whole(),
        scratch_shapes=[pltpu.VMEM((count, 8, 128), jnp.float32)],
        compiler_params=pltpu.CompilerParams(vmem_limit_bytes=VMEM),
        name="across_mix",
    )(values)


def turn(device):
    weights, weight = {}, 1
    for axis in reversed(ROUND):
        weights[axis] = weight
        weight *= SIZES[AXES.index(axis)]
    place = 0
    for axis, size in zip(reversed(AXES), reversed(SIZES)):
        place = place + (device & (size - 1)) * weights[axis]
        device = device >> (size.bit_length() - 1)
    return place


def split(values):
    high = values.astype(jnp.bfloat16)
    rest = values - high.astype(jnp.float32)
    middle = rest.astype(jnp.bfloat16)
    low = (rest - middle.astype(jnp.float32)).astype(jnp.bfloat16)
    return high, middle, low


def factors(parts, others, axis):
    high, middle, low = parts
    left = jnp.concatenate([high, low, middle, high, middle, high], axis=axis)
    high, middle, low = others
    right = jnp.concatenate([low, high, middle, middle, high, high], axis=0)
    return left, right


def pick_kernel(picks_ref, values_ref, out_ref, taken):
    count, halves, rows, width = values_ref.shape
    tiles, _, slots, _ = taken.shape
    owners, _, each, _ = out_ref.shape
    shift = rows.bit_length() - 1
    flat = values_ref.reshape(count * halves * rows, width)

    def body(step, carry):
        first = turn(step * (2 * AT_ONCE))
        for number in range(AT_ONCE):
            tile = step * AT_ONCE + number
            for slot in range(slots):
                pair, place = number * 2 + slot // each, slot % each
                pick = picks_ref[place, step * (2 * AT_ONCE) + pair]
                row = jnp.maximum(pick, 0)
                at = (row >> shift) * (halves * rows) + (row & (rows - 1))
                for half in range(halves):
                    part = jnp.where(pick >= 0, flat[pl.ds(at + half * rows, 1), :], 0.0)
                    taken[tile, half, slot:slot + 1, :] = part
                    out_ref[first + turn(pair), half, place:place + 1, :] = part
        return carry

    lax.fori_loop(0, tiles // AT_ONCE, body, 0)
    panel = jnp.concatenate([taken[:, half].reshape(-1, 128) for half in range(halves)], axis=1)
    left, right = factors(split(panel.T), split(panel), 1)
    gram = jnp.dot(left, right, preferred_element_type=jnp.float32)
    each = gram.shape[0] // out_ref.shape[0]
    for owner in range(out_ref.shape[0]):
        for half in range(halves):
            out_ref[owner, halves, half * each:(half + 1) * each, :] = (
                gram[owner * each:(owner + 1) * each, half * 128:half * 128 + 128]
            )


def pick_rows(values, picks):
    halves = values.shape[1]
    slots, owners = picks.shape
    return pl.pallas_call(
        pick_kernel,
        out_shape=jax.ShapeDtypeStruct((owners, halves + 1, slots, 128), jnp.float32),
        in_specs=[whole(pltpu.SMEM), whole()],
        out_specs=whole(),
        scratch_shapes=[pltpu.VMEM((slots * owners // TILE, halves, TILE, 128), jnp.float32)],
        compiler_params=pltpu.CompilerParams(vmem_limit_bytes=SMALL),
        name="pick_rows",
    )(picks, values)


def finish_kernel(expected, pieces_ref, received_ref, values_ref, mixed_ref, panel_ref, out_ref, held, panel, sems):
    size = held.shape[0]
    halves = size // 128
    each = pieces_ref.shape[1] // halves
    copies = [
        pltpu.make_async_copy(
            values_ref.at[:, half], mixed_ref.at[:, :, half * 128:half * 128 + 128], sems.at[half]
        )
        for half in range(halves)
    ]
    copies.append(pltpu.make_async_copy(panel, panel_ref, sems.at[halves]))
    for copy in copies[:halves]:
        copy.start()
    sources, _, slots, _ = received_ref.shape

    def move_rows(owner):
        for half in range(halves):
            held[owner * each:(owner + 1) * each, half * 128:half * 128 + 128] = (
                pieces_ref[owner, half * each:(half + 1) * each, :] * (1.0 / expected)
            )

    def move_panel(source):
        for half in range(halves):
            panel[source * slots:(source + 1) * slots, half * 128:half * 128 + 128] = (
                received_ref[turn(source), half]
            )

    first_owners = SUPER // each
    for owner in range(first_owners):
        move_rows(owner)
    moves = [(move_rows, owner) for owner in range(first_owners, pieces_ref.shape[0])]
    moves += [(move_panel, source) for source in range(sources)]

    place = lax.broadcasted_iota(jnp.int32, (TILE, 128), 0)
    lane = lax.broadcasted_iota(jnp.int32, (TILE, 128), 1)

    def spread_row(value, row):
        return jnp.broadcast_to(value[row:row + 1, :], (TILE, 128))

    def spread_column(value, column):
        return jnp.broadcast_to(value[:, column:column + 1], (TILE, 128))

    for base in range(0, size, SUPER):
        tiles = SUPER // TILE
        rows = [
            [held[base + t * TILE:base + (t + 1) * TILE, h * 128:h * 128 + 128] for h in range(halves)]
            for t in range(tiles)
        ]
        for t in range(tiles):
            first = base + t * TILE
            half, column = first // 128, first % 128
            edges = {
                u: [spread_column(rows[u][half], column + k) for k in range(TILE)]
                for u in range(t, tiles)
            }
            finished = list(rows[t])
            for k in range(TILE):
                for move, number in moves[:MOVES]:
                    move(number)
                moves = moves[MOVES:]
                pivot = spread_row(edges[t][k], k)
                inverse = 1.0 / pivot
                root = lax.rsqrt(pivot)
                root = root * (1.5 - 0.5 * pivot * root * root)
                lines = [spread_row(rows[t][h], k) for h in range(halves)]
                finished = [
                    jnp.where(place == k, lines[h] * root, finished[h]) for h in range(halves)
                ]
                lines = [line * inverse for line in lines]
                weights = [None] * TILE
                for m in range(k + 1, TILE):
                    weights[m] = spread_row(edges[t][k], m) * inverse
                for u in range(t, tiles):
                    edge = edges[u][k]
                    for m in range(k + 1, TILE):
                        edges[u][m] = edges[u][m] - edge * weights[m]
                    for h in range(halves):
                        rows[u][h] = rows[u][h] - edge * lines[h]
            rows[t] = [
                jnp.where(lane + h * 128 >= first + place, finished[h], 0.0) for h in range(halves)
            ]
            for h in range(halves):
                out_ref[first:first + TILE, h * 128:h * 128 + 128] = rows[t][h]
        if base == 0:
            for move, number in moves:
                move(number)
            moves = []
            copies[halves].start()
        after = base + SUPER
        if after < size:
            block = jnp.concatenate(
                [jnp.concatenate(rows[t], axis=1) for t in range(tiles)], axis=0
            )
            left, right = factors(split(block), split(block), 0)
            held[after:, :] -= jnp.dot(left.T[after:], right, preferred_element_type=jnp.float32)
    for copy in copies:
        copy.wait()


def finish(pieces, received, values, expected):
    owners, rows, width = pieces.shape
    count, halves, share, _ = values.shape
    size = halves * width
    panel = jax.ShapeDtypeStruct((received.shape[0] * received.shape[2], size), jnp.float32)
    return pl.pallas_call(
        lambda *refs: finish_kernel(expected, *refs),
        out_shape=(
            jax.ShapeDtypeStruct((count, share, size), jnp.float32),
            panel,
            jax.ShapeDtypeStruct((size, size), jnp.float32),
        ),
        in_specs=[whole()] * 3,
        out_specs=(whole(pltpu.HBM), whole(pltpu.HBM), whole()),
        scratch_shapes=[
            pltpu.VMEM((size, size), jnp.float32),
            pltpu.VMEM(panel.shape, jnp.float32),
            pltpu.SemaphoreType.DMA((halves + 1,)),
        ],
        compiler_params=pltpu.CompilerParams(vmem_limit_bytes=SMALL),
        name="finish",
    )(pieces, received, values)


def exchange(block):
    return lax.all_to_all(block, ROUND, split_axis=0, concat_axis=0, tiled=True)


def on_device(matrix_rows, signs, picks):
    length, width = matrix_rows.shape
    owners = math.prod(SIZES)
    slots = picks.shape[2]
    scale = 1.0 / math.sqrt(length * owners)
    expected = owners * owners * slots / 2.0

    values = exchange(across_mix(exchange(local_mix(matrix_rows, signs, scale, owners))))
    received = exchange(pick_rows(values, picks[0].T))
    piece = jnp.sum(received[:, -1], axis=0)
    pieces = exchange(jnp.broadcast_to(piece, (owners,) + piece.shape))
    mixed, panel, factor = finish(pieces, received, values, expected)
    return (mixed.reshape(length, width), panel, factor)


def solution(mesh):
    placed = (P(AXES, None), P(AXES), P(AXES, None, None))
    return jax.shard_map(
        on_device,
        mesh=Mesh(mesh.devices.reshape(SIZES), AXES),
        in_specs=placed,
        out_specs=(P(AXES, None), P(AXES, None), P()),
        check_vma=False,
    )
```

```python
import math

import jax
import jax.numpy as jnp
from jax import lax
from jax.experimental import pallas as pl
from jax.experimental.pallas import tpu as pltpu
from jax.sharding import Mesh, PartitionSpec as P

AXES = ("y_low", "x", "z", "core", "y_high")
SIZES = (2, 4, 4, 2, 2)
ROUND = ("z", "core", "x", "y_high", "y_low")
TILE = 8
RADIX = 8
AT_ONCE = 16
MOVES = 4
SUPER = 64
VMEM = 40 * 2**20
SMALL = 16 * 2**20
LARGE = 48 * 2**20


def butterflies(parts):
    count = len(parts)
    stride = 1
    while stride < count:
        for low in range(count):
            if low & stride == 0:
                first, second = parts[low], parts[low | stride]
                parts[low], parts[low | stride] = first + second, first - second
        stride *= 2
    return parts


def whole(space=pltpu.VMEM):
    return pl.BlockSpec(memory_space=space)


def local_kernel(scale, matrix_ref, signs_ref, out_ref, came, first, second, third, flips, signs_held, sems):
    halves, length, _ = came.shape
    share = out_ref.shape[2]
    size = length // RADIX
    group = TILE * RADIX
    loads = [
        [
            pltpu.make_async_copy(
                matrix_ref.at[pl.ds(c * size, size), h * 128:h * 128 + 128],
                came.at[h, pl.ds(c * size, size)],
                sems.at[c * halves + h],
            )
            for h in range(halves)
        ]
        for c in range(RADIX)
    ]
    signs_load = pltpu.make_async_copy(signs_ref, signs_held, sems.at[RADIX * halves])
    signs_load.start()
    for pair in loads:
        for load in pair:
            load.start()

    row = lax.broadcasted_iota(jnp.int32, (128, 128), 0)
    column = lax.broadcasted_iota(jnp.int32, (128, 128), 1)
    chosen = (row // 64 * 64 + row % 8 * 8 + row // 8 % 8 == column).astype(jnp.float32)
    ones = jnp.ones((128, 128), jnp.bfloat16)
    signs_load.wait()

    def flip(line, carry):
        signs = (2 * signs_held[pl.ds(line, 1), :] - 1).astype(jnp.float32)
        flips[pl.ds(pl.multiple_of(line * 128, 128), 128), :] = scale * jnp.dot(
            (chosen * signs).astype(jnp.bfloat16), ones, preferred_element_type=jnp.float32
        )
        return carry

    lax.fori_loop(0, length // 128, flip, 0, unroll=16)

    for c in range(RADIX):
        for load in loads[c]:
            load.wait()

        def inner(g, carry):
            base = pl.multiple_of(c * size + g * group, group)
            signs = [flips[pl.ds(base + TILE * s, TILE), :] for s in range(TILE)]
            for h in range(halves):
                parts = [came[h, pl.ds(base + s, RADIX, stride=TILE), :] * signs[s] for s in range(TILE)]
                parts = butterflies(parts)
                for s in range(TILE):
                    first[h, pl.ds(base + s, RADIX, stride=TILE), :] = parts[s]
            for h in range(halves):
                parts = butterflies([first[h, pl.ds(base + TILE * t, TILE), :] for t in range(RADIX)])
                for t in range(RADIX):
                    second[h, pl.ds(base + TILE * t, TILE), :] = parts[t]
            return carry

        lax.fori_loop(0, size // group, inner, 0, unroll=8)

        def outer(t, carry):
            base = pl.multiple_of(c * size + t * TILE, TILE)
            for h in range(halves):
                parts = butterflies([second[h, pl.ds(base + group * g, TILE), :] for g in range(size // group)])
                for g in range(size // group):
                    third[h, pl.ds(base + group * g, TILE), :] = parts[g]
            return carry

        lax.fori_loop(0, group // TILE, outer, 0, unroll=8)

    def last(q, carry):
        for t in range(share // TILE):
            for h in range(halves):
                at = pl.multiple_of(q * share, share) + t * TILE
                parts = butterflies([third[h, pl.ds(c * size + at, TILE), :] for c in range(RADIX)])
                for c in range(RADIX):
                    out_ref[c, q, t * TILE:(t + 1) * TILE, h * 128:h * 128 + 128] = parts[c]
        return carry

    lax.fori_loop(0, size // share, last, 0, unroll=2)


def local_mix(matrix_rows, signs, scale, owners):
    length, width = matrix_rows.shape
    halves = width // 128
    shape = (RADIX, owners // RADIX, length // owners, width)
    mixed = pl.pallas_call(
        lambda *refs: local_kernel(scale, *refs),
        out_shape=jax.ShapeDtypeStruct(shape, jnp.float32),
        in_specs=[whole(pltpu.HBM)] * 2,
        out_specs=whole(),
        scratch_shapes=[pltpu.VMEM((halves, length, 128), jnp.float32)] * 4
        + [
            pltpu.VMEM((length, 128), jnp.float32),
            pltpu.VMEM((length // 128, 128), jnp.int32),
            pltpu.SemaphoreType.DMA((RADIX * halves + 1,)),
        ],
        compiler_params=pltpu.CompilerParams(vmem_limit_bytes=LARGE),
        name="local_mix",
    )(matrix_rows, signs.reshape(length // 128, 128))
    return mixed.reshape(owners, length // owners, width)


def across_kernel(in_ref, out_ref, held):
    count, rows, width = in_ref.shape
    inner = 8
    outer = count // inner

    def body(tile, carry):
        at = pl.multiple_of(tile * 8, 8)
        for half in range(width // 128):
            columns = slice(half * 128, half * 128 + 128)
            for group in range(inner):
                parts = butterflies([in_ref[b * inner + group, pl.ds(at, 8), columns] for b in range(outer)])
                for b in range(outer):
                    held[b * inner + group] = parts[b]
            for group in range(outer):
                parts = butterflies([held[group * inner + b] for b in range(inner)])
                for b in range(inner):
                    out_ref[group * inner + b, half, pl.ds(at, 8), :] = parts[b]
        return carry

    lax.fori_loop(0, rows // 8, body, 0)


def across_mix(values):
    count, rows, width = values.shape
    return pl.pallas_call(
        across_kernel,
        out_shape=jax.ShapeDtypeStruct((count, width // 128, rows, 128), jnp.float32),
        in_specs=[whole()],
        out_specs=whole(),
        scratch_shapes=[pltpu.VMEM((count, 8, 128), jnp.float32)],
        compiler_params=pltpu.CompilerParams(vmem_limit_bytes=VMEM),
        name="across_mix",
    )(values)


def turn(device):
    weights, weight = {}, 1
    for axis in reversed(ROUND):
        weights[axis] = weight
        weight *= SIZES[AXES.index(axis)]
    place = 0
    for axis, size in zip(reversed(AXES), reversed(SIZES)):
        place = place + (device & (size - 1)) * weights[axis]
        device = device >> (size.bit_length() - 1)
    return place


def split(values):
    high = values.astype(jnp.bfloat16)
    rest = values - high.astype(jnp.float32)
    middle = rest.astype(jnp.bfloat16)
    low = (rest - middle.astype(jnp.float32)).astype(jnp.bfloat16)
    return high, middle, low


def factors(parts, others, axis):
    high, middle, low = parts
    left = jnp.concatenate([high, low, middle, high, middle, high], axis=axis)
    high, middle, low = others
    right = jnp.concatenate([low, high, middle, middle, high, high], axis=0)
    return left, right


def pick_kernel(picks_ref, values_ref, out_ref, taken):
    count, halves, rows, width = values_ref.shape
    tiles, _, slots, _ = taken.shape
    owners, _, each, _ = out_ref.shape
    shift = rows.bit_length() - 1
    flat = values_ref.reshape(count * halves * rows, width)

    def body(step, carry):
        first = turn(step * (2 * AT_ONCE))
        for number in range(AT_ONCE):
            tile = step * AT_ONCE + number
            for slot in range(slots):
                pair, place = number * 2 + slot // each, slot % each
                pick = picks_ref[place, step * (2 * AT_ONCE) + pair]
                row = jnp.maximum(pick, 0)
                at = (row >> shift) * (halves * rows) + (row & (rows - 1))
                for half in range(halves):
                    part = jnp.where(pick >= 0, flat[pl.ds(at + half * rows, 1), :], 0.0)
                    taken[tile, half, slot:slot + 1, :] = part
                    out_ref[first + turn(pair), half, place:place + 1, :] = part
        return carry

    lax.fori_loop(0, tiles // AT_ONCE, body, 0)
    panel = jnp.concatenate([taken[:, half].reshape(-1, 128) for half in range(halves)], axis=1)
    left, right = factors(split(panel.T), split(panel), 1)
    gram = jnp.dot(left, right, preferred_element_type=jnp.float32)
    each = gram.shape[0] // out_ref.shape[0]
    for owner in range(out_ref.shape[0]):
        for half in range(halves):
            out_ref[owner, halves, half * each:(half + 1) * each, :] = (
                gram[owner * each:(owner + 1) * each, half * 128:half * 128 + 128]
            )


def pick_rows(values, picks):
    halves = values.shape[1]
    slots, owners = picks.shape
    return pl.pallas_call(
        pick_kernel,
        out_shape=jax.ShapeDtypeStruct((owners, halves + 1, slots, 128), jnp.float32),
        in_specs=[whole(pltpu.SMEM), whole()],
        out_specs=whole(),
        scratch_shapes=[pltpu.VMEM((slots * owners // TILE, halves, TILE, 128), jnp.float32)],
        compiler_params=pltpu.CompilerParams(vmem_limit_bytes=SMALL),
        name="pick_rows",
    )(picks, values)


def finish_kernel(expected, pieces_ref, received_ref, values_ref, mixed_ref, panel_ref, out_ref, held, panel, sems):
    size = held.shape[0]
    halves = size // 128
    each = pieces_ref.shape[1] // halves
    copies = [
        pltpu.make_async_copy(
            values_ref.at[:, half], mixed_ref.at[:, :, half * 128:half * 128 + 128], sems.at[half]
        )
        for half in range(halves)
    ]
    copies.append(pltpu.make_async_copy(panel, panel_ref, sems.at[halves]))
    for copy in copies[:halves]:
        copy.start()
    sources, _, slots, _ = received_ref.shape

    def move_rows(owner):
        for half in range(halves):
            held[owner * each:(owner + 1) * each, half * 128:half * 128 + 128] = (
                pieces_ref[owner, half * each:(half + 1) * each, :] * (1.0 / expected)
            )

    def move_panel(source):
        for half in range(halves):
            panel[source * slots:(source + 1) * slots, half * 128:half * 128 + 128] = (
                received_ref[turn(source), half]
            )

    first_owners = SUPER // each
    for owner in range(first_owners):
        move_rows(owner)
    moves = [(move_rows, owner) for owner in range(first_owners, pieces_ref.shape[0])]
    moves += [(move_panel, source) for source in range(sources)]

    place = lax.broadcasted_iota(jnp.int32, (TILE, 128), 0)
    lane = lax.broadcasted_iota(jnp.int32, (TILE, 128), 1)

    def spread_row(value, row):
        return jnp.broadcast_to(value[row:row + 1, :], (TILE, 128))

    def spread_column(value, column):
        return jnp.broadcast_to(value[:, column:column + 1], (TILE, 128))

    for base in range(0, size, SUPER):
        tiles = SUPER // TILE
        rows = [
            [held[base + t * TILE:base + (t + 1) * TILE, h * 128:h * 128 + 128] for h in range(halves)]
            for t in range(tiles)
        ]
        for t in range(tiles):
            first = base + t * TILE
            half, column = first // 128, first % 128
            edges = {
                u: [spread_column(rows[u][half], column + k) for k in range(TILE)]
                for u in range(t, tiles)
            }
            finished = list(rows[t])
            for k in range(TILE):
                for move, number in moves[:MOVES]:
                    move(number)
                moves = moves[MOVES:]
                pivot = spread_row(edges[t][k], k)
                inverse = 1.0 / pivot
                root = lax.rsqrt(pivot)
                root = root * (1.5 - 0.5 * pivot * root * root)
                lines = [spread_row(rows[t][h], k) for h in range(halves)]
                finished = [
                    jnp.where(place == k, lines[h] * root, finished[h]) for h in range(halves)
                ]
                lines = [line * inverse for line in lines]
                weights = [None] * TILE
                for m in range(k + 1, TILE):
                    weights[m] = spread_row(edges[t][k], m) * inverse
                for u in range(t, tiles):
                    edge = edges[u][k]
                    for m in range(k + 1, TILE):
                        edges[u][m] = edges[u][m] - edge * weights[m]
                    for h in range(halves):
                        rows[u][h] = rows[u][h] - edge * lines[h]
            rows[t] = [
                jnp.where(lane + h * 128 >= first + place, finished[h], 0.0) for h in range(halves)
            ]
            for h in range(halves):
                out_ref[first:first + TILE, h * 128:h * 128 + 128] = rows[t][h]
        if base == 0:
            for move, number in moves:
                move(number)
            moves = []
            copies[halves].start()
        after = base + SUPER
        if after < size:
            block = jnp.concatenate(
                [jnp.concatenate(rows[t], axis=1) for t in range(tiles)], axis=0
            )
            left, right = factors(split(block), split(block), 0)
            held[after:, :] -= jnp.dot(left.T[after:], right, preferred_element_type=jnp.float32)
    for copy in copies:
        copy.wait()


def finish(pieces, received, values, expected):
    owners, rows, width = pieces.shape
    count, halves, share, _ = values.shape
    size = halves * width
    panel = jax.ShapeDtypeStruct((received.shape[0] * received.shape[2], size), jnp.float32)
    return pl.pallas_call(
        lambda *refs: finish_kernel(expected, *refs),
        out_shape=(
            jax.ShapeDtypeStruct((count, share, size), jnp.float32),
            panel,
            jax.ShapeDtypeStruct((size, size), jnp.float32),
        ),
        in_specs=[whole()] * 3,
        out_specs=(whole(pltpu.HBM), whole(pltpu.HBM), whole()),
        scratch_shapes=[
            pltpu.VMEM((size, size), jnp.float32),
            pltpu.VMEM(panel.shape, jnp.float32),
            pltpu.SemaphoreType.DMA((halves + 1,)),
        ],
        compiler_params=pltpu.CompilerParams(vmem_limit_bytes=SMALL),
        name="finish",
    )(pieces, received, values)


def exchange(block):
    return lax.all_to_all(block, ROUND, split_axis=0, concat_axis=0, tiled=True)


def on_device(matrix_rows, signs, picks):
    length, width = matrix_rows.shape
    owners = math.prod(SIZES)
    slots = picks.shape[2]
    scale = 1.0 / math.sqrt(length * owners)
    expected = owners * owners * slots / 2.0

    values = exchange(across_mix(exchange(local_mix(matrix_rows, signs, scale, owners))))
    received = exchange(pick_rows(values, picks[0].T))
    piece = jnp.sum(received[:, -1], axis=0)
    pieces = exchange(jnp.broadcast_to(piece, (owners,) + piece.shape))
    mixed, panel, factor = finish(pieces, received, values, expected)
    return (mixed.reshape(length, width), panel, factor)


def solution(mesh):
    placed = (P(AXES, None), P(AXES), P(AXES, None, None))
    return jax.shard_map(
        on_device,
        mesh=Mesh(mesh.devices.reshape(SIZES), AXES),
        in_specs=placed,
        out_specs=(P(AXES, None), P(AXES, None), P()),
        check_vma=False,
    )
```

```python
import math

import jax
import jax.numpy as jnp
from jax import lax
from jax.experimental import pallas as pl
from jax.experimental.pallas import tpu as pltpu
from jax.sharding import Mesh, PartitionSpec as P

AXES = ("y_low", "x", "z", "core", "y_high")
SIZES = (2, 4, 4, 2, 2)
ROUND = ("z", "core", "x", "y_high", "y_low")
TILE = 8
RADIX = 8
AT_ONCE = 16
MOVES = 4
SUPER = 64
VMEM = 40 * 2**20
SMALL = 16 * 2**20
LARGE = 48 * 2**20


def butterflies(parts):
    count = len(parts)
    stride = 1
    while stride < count:
        for low in range(count):
            if low & stride == 0:
                first, second = parts[low], parts[low | stride]
                parts[low], parts[low | stride] = first + second, first - second
        stride *= 2
    return parts


def whole(space=pltpu.VMEM):
    return pl.BlockSpec(memory_space=space)


def local_kernel(scale, matrix_ref, signs_ref, out_ref, came, first, second, third, flips, signs_held, sems):
    halves, length, _ = came.shape
    share = out_ref.shape[2]
    size = length // RADIX
    group = TILE * RADIX
    loads = [
        [
            pltpu.make_async_copy(
                matrix_ref.at[pl.ds(c * size, size), h * 128:h * 128 + 128],
                came.at[h, pl.ds(c * size, size)],
                sems.at[c * halves + h],
            )
            for h in range(halves)
        ]
        for c in range(RADIX)
    ]
    signs_load = pltpu.make_async_copy(signs_ref, signs_held, sems.at[RADIX * halves])
    signs_load.start()
    for pair in loads:
        for load in pair:
            load.start()

    row = lax.broadcasted_iota(jnp.int32, (128, 128), 0)
    column = lax.broadcasted_iota(jnp.int32, (128, 128), 1)
    chosen = (row // 64 * 64 + row % 8 * 8 + row // 8 % 8 == column).astype(jnp.float32)
    ones = jnp.ones((128, 128), jnp.bfloat16)
    signs_load.wait()

    def flip(line, carry):
        signs = (2 * signs_held[pl.ds(line, 1), :] - 1).astype(jnp.float32)
        flips[pl.ds(pl.multiple_of(line * 128, 128), 128), :] = scale * jnp.dot(
            (chosen * signs).astype(jnp.bfloat16), ones, preferred_element_type=jnp.float32
        )
        return carry

    lax.fori_loop(0, length // 128, flip, 0, unroll=16)

    for c in range(RADIX):
        for load in loads[c]:
            load.wait()

        def inner(g, carry):
            base = pl.multiple_of(c * size + g * group, group)
            signs = [flips[pl.ds(base + TILE * s, TILE), :] for s in range(TILE)]
            for h in range(halves):
                parts = [came[h, pl.ds(base + s, RADIX, stride=TILE), :] * signs[s] for s in range(TILE)]
                parts = butterflies(parts)
                for s in range(TILE):
                    first[h, pl.ds(base + s, RADIX, stride=TILE), :] = parts[s]
            for h in range(halves):
                parts = butterflies([first[h, pl.ds(base + TILE * t, TILE), :] for t in range(RADIX)])
                for t in range(RADIX):
                    second[h, pl.ds(base + TILE * t, TILE), :] = parts[t]
            return carry

        lax.fori_loop(0, size // group, inner, 0, unroll=8)

        def outer(t, carry):
            base = pl.multiple_of(c * size + t * TILE, TILE)
            for h in range(halves):
                parts = butterflies([second[h, pl.ds(base + group * g, TILE), :] for g in range(size // group)])
                for g in range(size // group):
                    third[h, pl.ds(base + group * g, TILE), :] = parts[g]
            return carry

        lax.fori_loop(0, group // TILE, outer, 0, unroll=8)

    def last(q, carry):
        for t in range(share // TILE):
            for h in range(halves):
                at = pl.multiple_of(q * share, share) + t * TILE
                parts = butterflies([third[h, pl.ds(c * size + at, TILE), :] for c in range(RADIX)])
                for c in range(RADIX):
                    out_ref[c, q, t * TILE:(t + 1) * TILE, h * 128:h * 128 + 128] = parts[c]
        return carry

    lax.fori_loop(0, size // share, last, 0, unroll=2)


def local_mix(matrix_rows, signs, scale, owners):
    length, width = matrix_rows.shape
    halves = width // 128
    shape = (RADIX, owners // RADIX, length // owners, width)
    mixed = pl.pallas_call(
        lambda *refs: local_kernel(scale, *refs),
        out_shape=jax.ShapeDtypeStruct(shape, jnp.float32),
        in_specs=[whole(pltpu.HBM)] * 2,
        out_specs=whole(),
        scratch_shapes=[pltpu.VMEM((halves, length, 128), jnp.float32)] * 4
        + [
            pltpu.VMEM((length, 128), jnp.float32),
            pltpu.VMEM((length // 128, 128), jnp.int32),
            pltpu.SemaphoreType.DMA((RADIX * halves + 1,)),
        ],
        compiler_params=pltpu.CompilerParams(vmem_limit_bytes=LARGE),
        name="local_mix",
    )(matrix_rows, signs.reshape(length // 128, 128))
    return mixed.reshape(owners, length // owners, width)


def across_kernel(in_ref, out_ref, held):
    count, rows, width = in_ref.shape
    inner = 8
    outer = count // inner

    def body(tile, carry):
        at = pl.multiple_of(tile * 8, 8)
        for half in range(width // 128):
            columns = slice(half * 128, half * 128 + 128)
            for group in range(inner):
                parts = butterflies([in_ref[b * inner + group, pl.ds(at, 8), columns] for b in range(outer)])
                for b in range(outer):
                    held[b * inner + group] = parts[b]
            for group in range(outer):
                parts = butterflies([held[group * inner + b] for b in range(inner)])
                for b in range(inner):
                    out_ref[group * inner + b, half, pl.ds(at, 8), :] = parts[b]
        return carry

    lax.fori_loop(0, rows // 8, body, 0)


def across_mix(values):
    count, rows, width = values.shape
    return pl.pallas_call(
        across_kernel,
        out_shape=jax.ShapeDtypeStruct((count, width // 128, rows, 128), jnp.float32),
        in_specs=[whole()],
        out_specs=whole(),
        scratch_shapes=[pltpu.VMEM((count, 8, 128), jnp.float32)],
        compiler_params=pltpu.CompilerParams(vmem_limit_bytes=VMEM),
        name="across_mix",
    )(values)


def turn(device):
    weights, weight = {}, 1
    for axis in reversed(ROUND):
        weights[axis] = weight
        weight *= SIZES[AXES.index(axis)]
    place = 0
    for axis, size in zip(reversed(AXES), reversed(SIZES)):
        place = place + (device & (size - 1)) * weights[axis]
        device = device >> (size.bit_length() - 1)
    return place


def split(values):
    high = values.astype(jnp.bfloat16)
    rest = values - high.astype(jnp.float32)
    middle = rest.astype(jnp.bfloat16)
    low = (rest - middle.astype(jnp.float32)).astype(jnp.bfloat16)
    return high, middle, low


def factors(parts, others, axis):
    high, middle, low = parts
    left = jnp.concatenate([high, low, middle, high, middle, high], axis=axis)
    high, middle, low = others
    right = jnp.concatenate([low, high, middle, middle, high, high], axis=0)
    return left, right


def pick_kernel(picks_ref, values_ref, out_ref, taken):
    count, halves, rows, width = values_ref.shape
    tiles, _, slots, _ = taken.shape
    owners = out_ref.shape[0]
    each = picks_ref.shape[0]
    shift = rows.bit_length() - 1
    flat = values_ref.reshape(count * halves * rows, width)

    def body(step, carry):
        first = turn(step * (2 * AT_ONCE))
        for number in range(AT_ONCE):
            tile = step * AT_ONCE + number
            for slot in range(slots):
                pair, place = number * 2 + slot // each, slot % each
                pick = picks_ref[place, step * (2 * AT_ONCE) + pair]
                row = jnp.maximum(pick, 0)
                at = (row >> shift) * (halves * rows) + (row & (rows - 1))
                for half in range(halves):
                    part = jnp.where(pick >= 0, flat[pl.ds(at + half * rows, 1), :], 0.0)
                    taken[tile, half, slot:slot + 1, :] = part
                    out_ref[first + turn(pair), half * each + place] = part
        return carry

    lax.fori_loop(0, tiles // AT_ONCE, body, 0)
    panel = jnp.concatenate([taken[:, half].reshape(-1, 128) for half in range(halves)], axis=1)
    left, right = factors(split(panel.T), split(panel), 1)
    gram = jnp.dot(left, right, preferred_element_type=jnp.float32)
    for owner in range(owners):
        line = halves * each
        for top in range(halves):
            for half in range(top, halves):
                row = top * width + owner
                out_ref[owner, line] = gram[row:row + 1, half * 128:half * 128 + 128]
                line += 1


def pick_rows(values, picks):
    halves = values.shape[1]
    slots, owners = picks.shape
    return pl.pallas_call(
        pick_kernel,
        out_shape=jax.ShapeDtypeStruct((owners, halves * slots + halves * (halves + 1) // 2, 1, 128), jnp.float32),
        in_specs=[whole(pltpu.SMEM), whole()],
        out_specs=whole(),
        scratch_shapes=[pltpu.VMEM((slots * owners // TILE, halves, TILE, 128), jnp.float32)],
        compiler_params=pltpu.CompilerParams(vmem_limit_bytes=SMALL),
        name="pick_rows",
    )(picks, values)


def finish_kernel(expected, pieces_ref, received_ref, values_ref, mixed_ref, panel_ref, out_ref, held, panel, sems):
    size = held.shape[0]
    halves = size // 128
    copies = [
        pltpu.make_async_copy(
            values_ref.at[:, half], mixed_ref.at[:, :, half * 128:half * 128 + 128], sems.at[half]
        )
        for half in range(halves)
    ]
    copies.append(pltpu.make_async_copy(panel, panel_ref, sems.at[halves]))
    for copy in copies[:halves]:
        copy.start()
    sources = received_ref.shape[0]
    slots = panel.shape[0] // sources

    def move_rows(owner):
        line = 0
        for top in range(halves):
            for half in range(top, halves):
                row = top * 128 + owner
                held[row:row + 1, half * 128:half * 128 + 128] = pieces_ref[owner, line] * (1.0 / expected)
                line += 1

    def move_panel(source):
        for half in range(halves):
            for slot in range(slots):
                row = source * slots + slot
                panel[row:row + 1, half * 128:half * 128 + 128] = received_ref[turn(source), half * slots + slot]

    held[128:, :128] = jnp.zeros((size - 128, 128), jnp.float32)

    first_owners = SUPER
    for owner in range(first_owners):
        move_rows(owner)
    moves = [(move_rows, owner) for owner in range(first_owners, pieces_ref.shape[0])]
    moves += [(move_panel, source) for source in range(sources)]

    place = lax.broadcasted_iota(jnp.int32, (TILE, 128), 0)
    lane = lax.broadcasted_iota(jnp.int32, (TILE, 128), 1)

    def spread_row(value, row):
        return jnp.broadcast_to(value[row:row + 1, :], (TILE, 128))

    def spread_column(value, column):
        return jnp.broadcast_to(value[:, column:column + 1], (TILE, 128))

    for base in range(0, size, SUPER):
        tiles = SUPER // TILE
        rows = [
            [held[base + t * TILE:base + (t + 1) * TILE, h * 128:h * 128 + 128] for h in range(halves)]
            for t in range(tiles)
        ]
        for t in range(tiles):
            first = base + t * TILE
            half, column = first // 128, first % 128
            edges = {
                u: [spread_column(rows[u][half], column + k) for k in range(TILE)]
                for u in range(t, tiles)
            }
            finished = list(rows[t])
            for k in range(TILE):
                for move, number in moves[:MOVES]:
                    move(number)
                moves = moves[MOVES:]
                pivot = spread_row(edges[t][k], k)
                inverse = 1.0 / pivot
                root = lax.rsqrt(pivot)
                root = root * (1.5 - 0.5 * pivot * root * root)
                lines = [spread_row(rows[t][h], k) for h in range(halves)]
                finished = [
                    jnp.where(place == k, lines[h] * root, finished[h]) for h in range(halves)
                ]
                lines = [line * inverse for line in lines]
                weights = [None] * TILE
                for m in range(k + 1, TILE):
                    weights[m] = spread_row(edges[t][k], m) * inverse
                for u in range(t, tiles):
                    edge = edges[u][k]
                    for m in range(k + 1, TILE):
                        edges[u][m] = edges[u][m] - edge * weights[m]
                    for h in range(halves):
                        rows[u][h] = rows[u][h] - edge * lines[h]
            rows[t] = [
                jnp.where(lane + h * 128 >= first + place, finished[h], 0.0) for h in range(halves)
            ]
            for h in range(halves):
                out_ref[first:first + TILE, h * 128:h * 128 + 128] = rows[t][h]
        if base == 0:
            for move, number in moves:
                move(number)
            moves = []
            copies[halves].start()
        after = base + SUPER
        if after < size:
            block = jnp.concatenate(
                [jnp.concatenate(rows[t], axis=1) for t in range(tiles)], axis=0
            )
            left, right = factors(split(block), split(block), 0)
            held[after:, :] -= jnp.dot(left.T[after:], right, preferred_element_type=jnp.float32)
    for copy in copies:
        copy.wait()


def finish(pieces, received, values, expected):
    count, halves, share, width = values.shape
    size = halves * width
    slots = (received.shape[1] - pieces.shape[1]) // halves
    panel = jax.ShapeDtypeStruct((received.shape[0] * slots, size), jnp.float32)
    return pl.pallas_call(
        lambda *refs: finish_kernel(expected, *refs),
        out_shape=(
            jax.ShapeDtypeStruct((count, share, size), jnp.float32),
            panel,
            jax.ShapeDtypeStruct((size, size), jnp.float32),
        ),
        in_specs=[whole()] * 3,
        out_specs=(whole(pltpu.HBM), whole(pltpu.HBM), whole()),
        scratch_shapes=[
            pltpu.VMEM((size, size), jnp.float32),
            pltpu.VMEM(panel.shape, jnp.float32),
            pltpu.SemaphoreType.DMA((halves + 1,)),
        ],
        compiler_params=pltpu.CompilerParams(vmem_limit_bytes=SMALL),
        name="finish",
    )(pieces, received, values)


def exchange(block):
    return lax.all_to_all(block, ROUND, split_axis=0, concat_axis=0, tiled=True)


def on_device(matrix_rows, signs, picks):
    length, width = matrix_rows.shape
    owners = math.prod(SIZES)
    slots = picks.shape[2]
    scale = 1.0 / math.sqrt(length * owners)
    expected = owners * owners * slots / 2.0

    values = exchange(across_mix(exchange(local_mix(matrix_rows, signs, scale, owners))))
    received = exchange(pick_rows(values, picks[0].T))
    piece = jnp.sum(received[:, slots * width // 128:], axis=0)
    pieces = exchange(jnp.broadcast_to(piece, (owners,) + piece.shape))
    mixed, panel, factor = finish(pieces, received, values, expected)
    return (mixed.reshape(length, width), panel, factor)


def solution(mesh):
    placed = (P(AXES, None), P(AXES), P(AXES, None, None))
    return jax.shard_map(
        on_device,
        mesh=Mesh(mesh.devices.reshape(SIZES), AXES),
        in_specs=placed,
        out_specs=(P(AXES, None), P(AXES, None), P()),
        check_vma=False,
    )
```

```python
import math

import jax
import jax.numpy as jnp
from jax import lax
from jax.experimental import pallas as pl
from jax.experimental.pallas import tpu as pltpu
from jax.sharding import Mesh, PartitionSpec as P

AXES = ("y_low", "x", "z", "core", "y_high")
SIZES = (2, 4, 4, 2, 2)
ROUND = ("z", "core", "x", "y_high", "y_low")
TILE = 8
RADIX = 8
AT_ONCE = 16
MOVES = 1
SUPER = 64
VMEM = 40 * 2**20
SMALL = 16 * 2**20
LARGE = 48 * 2**20


def butterflies(parts):
    count = len(parts)
    stride = 1
    while stride < count:
        for low in range(count):
            if low & stride == 0:
                first, second = parts[low], parts[low | stride]
                parts[low], parts[low | stride] = first + second, first - second
        stride *= 2
    return parts


def whole(space=pltpu.VMEM):
    return pl.BlockSpec(memory_space=space)


def local_kernel(scale, matrix_ref, signs_ref, out_ref, came, first, second, third, flips, signs_held, sems):
    halves, length, _ = came.shape
    share = out_ref.shape[2]
    size = length // RADIX
    group = TILE * RADIX
    loads = [
        [
            pltpu.make_async_copy(
                matrix_ref.at[pl.ds(c * size, size), h * 128:h * 128 + 128],
                came.at[h, pl.ds(c * size, size)],
                sems.at[c * halves + h],
            )
            for h in range(halves)
        ]
        for c in range(RADIX)
    ]
    signs_load = pltpu.make_async_copy(signs_ref, signs_held, sems.at[RADIX * halves])
    signs_load.start()
    for pair in loads:
        for load in pair:
            load.start()

    row = lax.broadcasted_iota(jnp.int32, (128, 128), 0)
    column = lax.broadcasted_iota(jnp.int32, (128, 128), 1)
    chosen = (row // 64 * 64 + row % 8 * 8 + row // 8 % 8 == column).astype(jnp.float32)
    ones = jnp.ones((128, 128), jnp.bfloat16)
    signs_load.wait()

    def flip(line, carry):
        signs = (2 * signs_held[pl.ds(line, 1), :] - 1).astype(jnp.float32)
        flips[pl.ds(pl.multiple_of(line * 128, 128), 128), :] = scale * jnp.dot(
            (chosen * signs).astype(jnp.bfloat16), ones, preferred_element_type=jnp.float32
        )
        return carry

    lax.fori_loop(0, length // 128, flip, 0, unroll=16)

    for c in range(RADIX):
        for load in loads[c]:
            load.wait()

        def inner(g, carry):
            base = pl.multiple_of(c * size + g * group, group)
            signs = [flips[pl.ds(base + TILE * s, TILE), :] for s in range(TILE)]
            for h in range(halves):
                parts = [came[h, pl.ds(base + s, RADIX, stride=TILE), :] * signs[s] for s in range(TILE)]
                parts = butterflies(parts)
                for s in range(TILE):
                    first[h, pl.ds(base + s, RADIX, stride=TILE), :] = parts[s]
            for h in range(halves):
                parts = butterflies([first[h, pl.ds(base + TILE * t, TILE), :] for t in range(RADIX)])
                for t in range(RADIX):
                    second[h, pl.ds(base + TILE * t, TILE), :] = parts[t]
            return carry

        lax.fori_loop(0, size // group, inner, 0, unroll=8)

        def outer(t, carry):
            base = pl.multiple_of(c * size + t * TILE, TILE)
            for h in range(halves):
                parts = butterflies([second[h, pl.ds(base + group * g, TILE), :] for g in range(size // group)])
                for g in range(size // group):
                    third[h, pl.ds(base + group * g, TILE), :] = parts[g]
            return carry

        lax.fori_loop(0, group // TILE, outer, 0, unroll=8)

    def last(q, carry):
        for t in range(share // TILE):
            for h in range(halves):
                at = pl.multiple_of(q * share, share) + t * TILE
                parts = butterflies([third[h, pl.ds(c * size + at, TILE), :] for c in range(RADIX)])
                for c in range(RADIX):
                    out_ref[c, q, t * TILE:(t + 1) * TILE, h * 128:h * 128 + 128] = parts[c]
        return carry

    lax.fori_loop(0, size // share, last, 0, unroll=2)


def local_mix(matrix_rows, signs, scale, owners):
    length, width = matrix_rows.shape
    halves = width // 128
    shape = (RADIX, owners // RADIX, length // owners, width)
    mixed = pl.pallas_call(
        lambda *refs: local_kernel(scale, *refs),
        out_shape=jax.ShapeDtypeStruct(shape, jnp.float32),
        in_specs=[whole(pltpu.HBM)] * 2,
        out_specs=whole(),
        scratch_shapes=[pltpu.VMEM((halves, length, 128), jnp.float32)] * 4
        + [
            pltpu.VMEM((length, 128), jnp.float32),
            pltpu.VMEM((length // 128, 128), jnp.int32),
            pltpu.SemaphoreType.DMA((RADIX * halves + 1,)),
        ],
        compiler_params=pltpu.CompilerParams(vmem_limit_bytes=LARGE),
        name="local_mix",
    )(matrix_rows, signs.reshape(length // 128, 128))
    return mixed.reshape(owners, length // owners, width)


def across_kernel(in_ref, out_ref, held):
    count, rows, width = in_ref.shape
    inner = 8
    outer = count // inner

    def body(tile, carry):
        at = pl.multiple_of(tile * 8, 8)
        for half in range(width // 128):
            columns = slice(half * 128, half * 128 + 128)
            for group in range(inner):
                parts = butterflies([in_ref[b * inner + group, pl.ds(at, 8), columns] for b in range(outer)])
                for b in range(outer):
                    held[b * inner + group] = parts[b]
            for group in range(outer):
                parts = butterflies([held[group * inner + b] for b in range(inner)])
                for b in range(inner):
                    out_ref[group * inner + b, half, pl.ds(at, 8), :] = parts[b]
        return carry

    lax.fori_loop(0, rows // 8, body, 0)


def across_mix(values):
    count, rows, width = values.shape
    return pl.pallas_call(
        across_kernel,
        out_shape=jax.ShapeDtypeStruct((count, width // 128, rows, 128), jnp.float32),
        in_specs=[whole()],
        out_specs=whole(),
        scratch_shapes=[pltpu.VMEM((count, 8, 128), jnp.float32)],
        compiler_params=pltpu.CompilerParams(vmem_limit_bytes=VMEM),
        name="across_mix",
    )(values)


def turn(device):
    weights, weight = {}, 1
    for axis in reversed(ROUND):
        weights[axis] = weight
        weight *= SIZES[AXES.index(axis)]
    place = 0
    for axis, size in zip(reversed(AXES), reversed(SIZES)):
        place = place + (device & (size - 1)) * weights[axis]
        device = device >> (size.bit_length() - 1)
    return place


def split(values):
    high = values.astype(jnp.bfloat16)
    rest = values - high.astype(jnp.float32)
    middle = rest.astype(jnp.bfloat16)
    low = (rest - middle.astype(jnp.float32)).astype(jnp.bfloat16)
    return high, middle, low


def factors(parts, others, axis):
    high, middle, low = parts
    left = jnp.concatenate([high, low, middle, high, middle, high], axis=axis)
    high, middle, low = others
    right = jnp.concatenate([low, high, middle, middle, high, high], axis=0)
    return left, right


def pick_kernel(picks_ref, values_ref, out_ref, taken):
    count, halves, rows, width = values_ref.shape
    tiles, _, slots, _ = taken.shape
    owners = out_ref.shape[0]
    each = picks_ref.shape[0]
    shift = rows.bit_length() - 1
    flat = values_ref.reshape(count * halves * rows, width)

    def body(step, carry):
        first = turn(step * (2 * AT_ONCE))
        for number in range(AT_ONCE):
            tile = step * AT_ONCE + number
            for slot in range(slots):
                pair, place = number * 2 + slot // each, slot % each
                pick = picks_ref[place, step * (2 * AT_ONCE) + pair]
                row = jnp.maximum(pick, 0)
                at = (row >> shift) * (halves * rows) + (row & (rows - 1))
                for half in range(halves):
                    part = jnp.where(pick >= 0, flat[pl.ds(at + half * rows, 1), :], 0.0)
                    taken[tile, half, slot:slot + 1, :] = part
                    out_ref[first + turn(pair), half * each + place] = part
        return carry

    lax.fori_loop(0, tiles // AT_ONCE, body, 0)
    panel = jnp.concatenate([taken[:, half].reshape(-1, 128) for half in range(halves)], axis=1)
    left, right = factors(split(panel.T), split(panel), 1)
    gram = jnp.dot(left, right, preferred_element_type=jnp.float32)
    for owner in range(owners):
        line = halves * each
        for top in range(halves):
            for half in range(top, halves):
                row = top * width + owner
                out_ref[owner, line] = gram[row:row + 1, half * 128:half * 128 + 128]
                line += 1


def pick_rows(values, picks):
    halves = values.shape[1]
    slots, owners = picks.shape
    return pl.pallas_call(
        pick_kernel,
        out_shape=jax.ShapeDtypeStruct((owners, halves * slots + halves * (halves + 1) // 2, 1, 128), jnp.float32),
        in_specs=[whole(pltpu.SMEM), whole()],
        out_specs=whole(),
        scratch_shapes=[pltpu.VMEM((slots * owners // TILE, halves, TILE, 128), jnp.float32)],
        compiler_params=pltpu.CompilerParams(vmem_limit_bytes=SMALL),
        name="pick_rows",
    )(picks, values)


def finish_kernel(expected, pieces_ref, received_ref, values_ref, mixed_ref, panel_ref, out_ref, held, panel, sems):
    size = held.shape[0]
    halves = size // 128
    copies = [
        pltpu.make_async_copy(
            values_ref.at[:, half], mixed_ref.at[:, :, half * 128:half * 128 + 128], sems.at[half]
        )
        for half in range(halves)
    ]
    copies.append(pltpu.make_async_copy(panel, panel_ref, sems.at[halves]))
    for copy in copies[:halves]:
        copy.start()
    sources = received_ref.shape[0]
    slots = panel.shape[0] // sources

    def move_rows(owner):
        line = 0
        for top in range(halves):
            for half in range(top, halves):
                row = top * 128 + owner
                held[row:row + 1, half * 128:half * 128 + 128] = pieces_ref[owner, line] * (1.0 / expected)
                line += 1

    def move_panel(source):
        for half in range(halves):
            for slot in range(slots):
                row = source * slots + slot
                panel[row:row + 1, half * 128:half * 128 + 128] = received_ref[turn(source), half * slots + slot]

    held[128:, :128] = jnp.zeros((size - 128, 128), jnp.float32)

    first_owners = SUPER
    for owner in range(first_owners):
        move_rows(owner)
    moves = [(move_rows, owner) for owner in range(first_owners, pieces_ref.shape[0])]
    moves += [(move_panel, source) for source in range(sources)]

    place = lax.broadcasted_iota(jnp.int32, (TILE, 128), 0)
    lane = lax.broadcasted_iota(jnp.int32, (TILE, 128), 1)

    def spread_row(value, row):
        return jnp.broadcast_to(value[row:row + 1, :], (TILE, 128))

    def spread_column(value, column):
        return jnp.broadcast_to(value[:, column:column + 1], (TILE, 128))

    for base in range(0, size, SUPER):
        tiles = SUPER // TILE
        rows = [
            [held[base + t * TILE:base + (t + 1) * TILE, h * 128:h * 128 + 128] for h in range(halves)]
            for t in range(tiles)
        ]
        for t in range(tiles):
            first = base + t * TILE
            half, column = first // 128, first % 128
            low = half
            edges = {
                u: [spread_column(rows[u][half], column + k) for k in range(TILE)]
                for u in range(t, tiles)
            }
            finished = list(rows[t])
            for k in range(TILE):
                for move, number in moves[:MOVES]:
                    move(number)
                moves = moves[MOVES:]
                pivot = spread_row(edges[t][k], k)
                inverse = 1.0 / pivot
                root = lax.rsqrt(pivot)
                root = root * (1.5 - 0.5 * pivot * root * root)
                lines = [spread_row(rows[t][h], k) if h >= low else rows[t][h] for h in range(halves)]
                finished = [
                    jnp.where(place == k, lines[h] * root, finished[h]) if h >= low else finished[h] for h in range(halves)
                ]
                lines = [line * inverse for line in lines]
                weights = [None] * TILE
                for m in range(k + 1, TILE):
                    weights[m] = spread_row(edges[t][k], m) * inverse
                for u in range(t, tiles):
                    edge = edges[u][k]
                    for m in range(k + 1, TILE):
                        edges[u][m] = edges[u][m] - edge * weights[m]
                    for h in range(low, halves):
                        rows[u][h] = rows[u][h] - edge * lines[h]
            rows[t] = [
                jnp.where(lane + h * 128 >= first + place, finished[h], 0.0) for h in range(halves)
            ]
            for h in range(halves):
                out_ref[first:first + TILE, h * 128:h * 128 + 128] = rows[t][h]
        if base == size // 2:
            for move, number in moves:
                move(number)
            moves = []
            copies[halves].start()
        after = base + SUPER
        if after < size:
            block = jnp.concatenate(
                [jnp.concatenate(rows[t], axis=1) for t in range(tiles)], axis=0
            )
            left, right = factors(split(block), split(block), 0)
            held[after:, :] -= jnp.dot(left.T[after:], right, preferred_element_type=jnp.float32)
    for copy in copies:
        copy.wait()


def finish(pieces, received, values, expected):
    count, halves, share, width = values.shape
    size = halves * width
    slots = (received.shape[1] - pieces.shape[1]) // halves
    panel = jax.ShapeDtypeStruct((received.shape[0] * slots, size), jnp.float32)
    return pl.pallas_call(
        lambda *refs: finish_kernel(expected, *refs),
        out_shape=(
            jax.ShapeDtypeStruct((count, share, size), jnp.float32),
            panel,
            jax.ShapeDtypeStruct((size, size), jnp.float32),
        ),
        in_specs=[whole()] * 3,
        out_specs=(whole(pltpu.HBM), whole(pltpu.HBM), whole()),
        scratch_shapes=[
            pltpu.VMEM((size, size), jnp.float32),
            pltpu.VMEM(panel.shape, jnp.float32),
            pltpu.SemaphoreType.DMA((halves + 1,)),
        ],
        compiler_params=pltpu.CompilerParams(vmem_limit_bytes=SMALL),
        name="finish",
    )(pieces, received, values)


def exchange(block):
    return lax.all_to_all(block, ROUND, split_axis=0, concat_axis=0, tiled=True)


def on_device(matrix_rows, signs, picks):
    length, width = matrix_rows.shape
    owners = math.prod(SIZES)
    slots = picks.shape[2]
    scale = 1.0 / math.sqrt(length * owners)
    expected = owners * owners * slots / 2.0

    values = exchange(across_mix(exchange(local_mix(matrix_rows, signs, scale, owners))))
    received = exchange(pick_rows(values, picks[0].T))
    piece = jnp.sum(received[:, slots * width // 128:], axis=0)
    pieces = exchange(jnp.broadcast_to(piece, (owners,) + piece.shape))
    mixed, panel, factor = finish(pieces, received, values, expected)
    return (mixed.reshape(length, width), panel, factor)


def solution(mesh):
    placed = (P(AXES, None), P(AXES), P(AXES, None, None))
    return jax.shard_map(
        on_device,
        mesh=Mesh(mesh.devices.reshape(SIZES), AXES),
        in_specs=placed,
        out_specs=(P(AXES, None), P(AXES, None), P()),
        check_vma=False,
    )
```

```python
import math

import jax
import jax.numpy as jnp
from jax import lax
from jax.experimental import pallas as pl
from jax.experimental.pallas import tpu as pltpu
from jax.sharding import Mesh, PartitionSpec as P

AXES = ("y_low", "x", "z", "core", "y_high")
SIZES = (2, 4, 4, 2, 2)
ROUND = ("z", "core", "x", "y_high", "y_low")
TILE = 8
RADIX = 8
AT_ONCE = 16
MOVES = 4
SUPER = 64
VMEM = 40 * 2**20
SMALL = 16 * 2**20
LARGE = 48 * 2**20


def butterflies(parts):
    count = len(parts)
    stride = 1
    while stride < count:
        for low in range(count):
            if low & stride == 0:
                first, second = parts[low], parts[low | stride]
                parts[low], parts[low | stride] = first + second, first - second
        stride *= 2
    return parts


def whole(space=pltpu.VMEM):
    return pl.BlockSpec(memory_space=space)


def local_kernel(scale, matrix_ref, signs_ref, out_ref, came, first, second, third, flips, signs_held, sems):
    halves, length, _ = came.shape
    share = out_ref.shape[2]
    size = length // RADIX
    group = TILE * RADIX
    loads = [
        [
            pltpu.make_async_copy(
                matrix_ref.at[pl.ds(c * size, size), h * 128:h * 128 + 128],
                came.at[h, pl.ds(c * size, size)],
                sems.at[c * halves + h],
            )
            for h in range(halves)
        ]
        for c in range(RADIX)
    ]
    signs_load = pltpu.make_async_copy(signs_ref, signs_held, sems.at[RADIX * halves])
    signs_load.start()
    for pair in loads:
        for load in pair:
            load.start()

    row = lax.broadcasted_iota(jnp.int32, (128, 128), 0)
    column = lax.broadcasted_iota(jnp.int32, (128, 128), 1)
    chosen = (row // 64 * 64 + row % 8 * 8 + row // 8 % 8 == column).astype(jnp.float32)
    ones = jnp.ones((128, 128), jnp.bfloat16)
    signs_load.wait()

    def flip(line, carry):
        signs = (2 * signs_held[pl.ds(line, 1), :] - 1).astype(jnp.float32)
        flips[pl.ds(pl.multiple_of(line * 128, 128), 128), :] = scale * jnp.dot(
            (chosen * signs).astype(jnp.bfloat16), ones, preferred_element_type=jnp.float32
        )
        return carry

    lax.fori_loop(0, length // 128, flip, 0, unroll=16)

    for c in range(RADIX):
        for load in loads[c]:
            load.wait()

        def inner(g, carry):
            base = pl.multiple_of(c * size + g * group, group)
            signs = [flips[pl.ds(base + TILE * s, TILE), :] for s in range(TILE)]
            for h in range(halves):
                parts = [came[h, pl.ds(base + s, RADIX, stride=TILE), :] * signs[s] for s in range(TILE)]
                parts = butterflies(parts)
                for s in range(TILE):
                    first[h, pl.ds(base + s, RADIX, stride=TILE), :] = parts[s]
            for h in range(halves):
                parts = butterflies([first[h, pl.ds(base + TILE * t, TILE), :] for t in range(RADIX)])
                for t in range(RADIX):
                    second[h, pl.ds(base + TILE * t, TILE), :] = parts[t]
            return carry

        lax.fori_loop(0, size // group, inner, 0, unroll=8)

        def outer(t, carry):
            base = pl.multiple_of(c * size + t * TILE, TILE)
            for h in range(halves):
                parts = butterflies([second[h, pl.ds(base + group * g, TILE), :] for g in range(size // group)])
                for g in range(size // group):
                    third[h, pl.ds(base + group * g, TILE), :] = parts[g]
            return carry

        lax.fori_loop(0, group // TILE, outer, 0, unroll=8)

    def last(q, carry):
        for t in range(share // TILE):
            for h in range(halves):
                at = pl.multiple_of(q * share, share) + t * TILE
                parts = butterflies([third[h, pl.ds(c * size + at, TILE), :] for c in range(RADIX)])
                for c in range(RADIX):
                    out_ref[c, q, t * TILE:(t + 1) * TILE, h * 128:h * 128 + 128] = parts[c]
        return carry

    lax.fori_loop(0, size // share, last, 0, unroll=4)


def local_mix(matrix_rows, signs, scale, owners):
    length, width = matrix_rows.shape
    halves = width // 128
    shape = (RADIX, owners // RADIX, length // owners, width)
    mixed = pl.pallas_call(
        lambda *refs: local_kernel(scale, *refs),
        out_shape=jax.ShapeDtypeStruct(shape, jnp.float32),
        in_specs=[whole(pltpu.HBM)] * 2,
        out_specs=whole(),
        scratch_shapes=[pltpu.VMEM((halves, length, 128), jnp.float32)] * 4
        + [
            pltpu.VMEM((length, 128), jnp.float32),
            pltpu.VMEM((length // 128, 128), jnp.int32),
            pltpu.SemaphoreType.DMA((RADIX * halves + 1,)),
        ],
        compiler_params=pltpu.CompilerParams(vmem_limit_bytes=LARGE),
        name="local_mix",
    )(matrix_rows, signs.reshape(length // 128, 128))
    return mixed.reshape(owners, length // owners, width)


def across_kernel(in_ref, out_ref, held):
    count, rows, width = in_ref.shape
    inner = 8
    outer = count // inner

    def body(tile, carry):
        at = pl.multiple_of(tile * 8, 8)
        for half in range(width // 128):
            columns = slice(half * 128, half * 128 + 128)
            for group in range(inner):
                parts = butterflies([in_ref[b * inner + group, pl.ds(at, 8), columns] for b in range(outer)])
                for b in range(outer):
                    held[b * inner + group] = parts[b]
            for group in range(outer):
                parts = butterflies([held[group * inner + b] for b in range(inner)])
                for b in range(inner):
                    out_ref[group * inner + b, half, pl.ds(at, 8), :] = parts[b]
        return carry

    lax.fori_loop(0, rows // 8, body, 0, unroll=4)


def across_mix(values):
    count, rows, width = values.shape
    return pl.pallas_call(
        across_kernel,
        out_shape=jax.ShapeDtypeStruct((count, width // 128, rows, 128), jnp.float32),
        in_specs=[whole()],
        out_specs=whole(),
        scratch_shapes=[pltpu.VMEM((count, 8, 128), jnp.float32)],
        compiler_params=pltpu.CompilerParams(vmem_limit_bytes=VMEM),
        name="across_mix",
    )(values)


def turn(device):
    weights, weight = {}, 1
    for axis in reversed(ROUND):
        weights[axis] = weight
        weight *= SIZES[AXES.index(axis)]
    place = 0
    for axis, size in zip(reversed(AXES), reversed(SIZES)):
        place = place + (device & (size - 1)) * weights[axis]
        device = device >> (size.bit_length() - 1)
    return place


def split(values):
    high = values.astype(jnp.bfloat16)
    rest = values - high.astype(jnp.float32)
    middle = rest.astype(jnp.bfloat16)
    low = (rest - middle.astype(jnp.float32)).astype(jnp.bfloat16)
    return high, middle, low


def factors(parts, others, axis):
    high, middle, low = parts
    left = jnp.concatenate([high, low, middle, high, middle, high], axis=axis)
    high, middle, low = others
    right = jnp.concatenate([low, high, middle, middle, high, high], axis=0)
    return left, right


def pick_kernel(picks_ref, values_ref, out_ref, taken):
    count, halves, rows, width = values_ref.shape
    tiles, _, slots, _ = taken.shape
    owners = out_ref.shape[0]
    each = picks_ref.shape[0]
    shift = rows.bit_length() - 1
    flat = values_ref.reshape(count * halves * rows, width)

    def body(step, carry):
        first = turn(step * (2 * AT_ONCE))
        for number in range(AT_ONCE):
            tile = step * AT_ONCE + number
            for slot in range(slots):
                pair, place = number * 2 + slot // each, slot % each
                pick = picks_ref[place, step * (2 * AT_ONCE) + pair]
                row = jnp.maximum(pick, 0)
                at = (row >> shift) * (halves * rows) + (row & (rows - 1))
                for half in range(halves):
                    part = jnp.where(pick >= 0, flat[pl.ds(at + half * rows, 1), :], 0.0)
                    taken[tile, half, slot:slot + 1, :] = part
                    out_ref[first + turn(pair), half * each + place] = part
        return carry

    lax.fori_loop(0, tiles // AT_ONCE, body, 0)
    panel = jnp.concatenate([taken[:, half].reshape(-1, 128) for half in range(halves)], axis=1)
    left, right = factors(split(panel.T), split(panel), 1)
    gram = jnp.dot(left, right, preferred_element_type=jnp.float32)
    for owner in range(owners):
        line = halves * each
        for top in range(halves):
            for half in range(top, halves):
                row = top * width + owner
                out_ref[owner, line] = gram[row:row + 1, half * 128:half * 128 + 128]
                line += 1


def pick_rows(values, picks):
    halves = values.shape[1]
    slots, owners = picks.shape
    return pl.pallas_call(
        pick_kernel,
        out_shape=jax.ShapeDtypeStruct((owners, halves * slots + halves * (halves + 1) // 2, 1, 128), jnp.float32),
        in_specs=[whole(pltpu.SMEM), whole()],
        out_specs=whole(),
        scratch_shapes=[pltpu.VMEM((slots * owners // TILE, halves, TILE, 128), jnp.float32)],
        compiler_params=pltpu.CompilerParams(vmem_limit_bytes=SMALL),
        name="pick_rows",
    )(picks, values)


def finish_kernel(expected, pieces_ref, received_ref, values_ref, mixed_ref, panel_ref, out_ref, held, panel, sems):
    size = held.shape[0]
    halves = size // 128
    copies = [
        pltpu.make_async_copy(
            values_ref.at[:, half], mixed_ref.at[:, :, half * 128:half * 128 + 128], sems.at[half]
        )
        for half in range(halves)
    ]
    copies.append(pltpu.make_async_copy(panel, panel_ref, sems.at[halves]))
    for copy in copies[:halves]:
        copy.start()
    sources = received_ref.shape[0]
    slots = panel.shape[0] // sources

    def move_rows(owner):
        line = 0
        for top in range(halves):
            for half in range(top, halves):
                row = top * 128 + owner
                held[row:row + 1, half * 128:half * 128 + 128] = pieces_ref[owner, line] * (1.0 / expected)
                line += 1

    def move_panel(source):
        for half in range(halves):
            for slot in range(slots):
                row = source * slots + slot
                panel[row:row + 1, half * 128:half * 128 + 128] = received_ref[turn(source), half * slots + slot]

    held[128:, :128] = jnp.zeros((size - 128, 128), jnp.float32)

    first_owners = SUPER
    for owner in range(first_owners):
        move_rows(owner)
    moves = [(move_rows, owner) for owner in range(first_owners, pieces_ref.shape[0])]
    moves += [(move_panel, source) for source in range(sources)]

    place = lax.broadcasted_iota(jnp.int32, (TILE, 128), 0)
    lane = lax.broadcasted_iota(jnp.int32, (TILE, 128), 1)

    def spread_row(value, row):
        return jnp.broadcast_to(value[row:row + 1, :], (TILE, 128))

    def spread_column(value, column):
        return jnp.broadcast_to(value[:, column:column + 1], (TILE, 128))

    for base in range(0, size, SUPER):
        tiles = SUPER // TILE
        rows = [
            [held[base + t * TILE:base + (t + 1) * TILE, h * 128:h * 128 + 128] for h in range(halves)]
            for t in range(tiles)
        ]
        for t in range(tiles):
            first = base + t * TILE
            half, column = first // 128, first % 128
            edges = {
                u: [spread_column(rows[u][half], column + k) for k in range(TILE)]
                for u in range(t, tiles)
            }
            finished = list(rows[t])
            for k in range(TILE):
                for move, number in moves[:MOVES]:
                    move(number)
                moves = moves[MOVES:]
                pivot = spread_row(edges[t][k], k)
                inverse = 1.0 / pivot
                root = lax.rsqrt(pivot)
                root = root * (1.5 - 0.5 * pivot * root * root)
                lines = [spread_row(rows[t][h], k) for h in range(halves)]
                finished = [
                    jnp.where(place == k, lines[h] * root, finished[h]) for h in range(halves)
                ]
                lines = [line * inverse for line in lines]
                weights = [None] * TILE
                for m in range(k + 1, TILE):
                    weights[m] = spread_row(edges[t][k], m) * inverse
                for u in range(t, tiles):
                    edge = edges[u][k]
                    for m in range(k + 1, TILE):
                        edges[u][m] = edges[u][m] - edge * weights[m]
                    for h in range(halves):
                        rows[u][h] = rows[u][h] - edge * lines[h]
            rows[t] = [
                jnp.where(lane + h * 128 >= first + place, finished[h], 0.0) for h in range(halves)
            ]
            for h in range(halves):
                out_ref[first:first + TILE, h * 128:h * 128 + 128] = rows[t][h]
        if base == 0:
            for move, number in moves:
                move(number)
            moves = []
            copies[halves].start()
        after = base + SUPER
        if after < size:
            block = jnp.concatenate(
                [jnp.concatenate(rows[t], axis=1) for t in range(tiles)], axis=0
            )
            left, right = factors(split(block), split(block), 0)
            held[after:, :] -= jnp.dot(left.T[after:], right, preferred_element_type=jnp.float32)
    for copy in copies:
        copy.wait()


def finish(pieces, received, values, expected):
    count, halves, share, width = values.shape
    size = halves * width
    slots = (received.shape[1] - pieces.shape[1]) // halves
    panel = jax.ShapeDtypeStruct((received.shape[0] * slots, size), jnp.float32)
    return pl.pallas_call(
        lambda *refs: finish_kernel(expected, *refs),
        out_shape=(
            jax.ShapeDtypeStruct((count, share, size), jnp.float32),
            panel,
            jax.ShapeDtypeStruct((size, size), jnp.float32),
        ),
        in_specs=[whole()] * 3,
        out_specs=(whole(pltpu.HBM), whole(pltpu.HBM), whole()),
        scratch_shapes=[
            pltpu.VMEM((size, size), jnp.float32),
            pltpu.VMEM(panel.shape, jnp.float32),
            pltpu.SemaphoreType.DMA((halves + 1,)),
        ],
        compiler_params=pltpu.CompilerParams(vmem_limit_bytes=SMALL),
        name="finish",
    )(pieces, received, values)


def exchange(block):
    return lax.all_to_all(block, ROUND, split_axis=0, concat_axis=0, tiled=True)


def on_device(matrix_rows, signs, picks):
    length, width = matrix_rows.shape
    owners = math.prod(SIZES)
    slots = picks.shape[2]
    scale = 1.0 / math.sqrt(length * owners)
    expected = owners * owners * slots / 2.0

    values = exchange(across_mix(exchange(local_mix(matrix_rows, signs, scale, owners))))
    received = exchange(pick_rows(values, picks[0].T))
    piece = jnp.sum(received[:, slots * width // 128:], axis=0)
    pieces = exchange(jnp.broadcast_to(piece, (owners,) + piece.shape))
    mixed, panel, factor = finish(pieces, received, values, expected)
    return (mixed.reshape(length, width), panel, factor)


def solution(mesh):
    placed = (P(AXES, None), P(AXES), P(AXES, None, None))
    return jax.shard_map(
        on_device,
        mesh=Mesh(mesh.devices.reshape(SIZES), AXES),
        in_specs=placed,
        out_specs=(P(AXES, None), P(AXES, None), P()),
        check_vma=False,
    )
```
